256 devices in a mesh: section: 32 (over x, z_hi, core), dp: 8 (over z_lo, y).
Axes of the slice: x: 4, y: 4, z: 8 (z_hi: 4, z_lo: 2; z = z_hi * 2 + z_lo), core: 2. Of those that a mesh axis runs over, the one named last changes fastest.
Arguments:
- x_fwd: bfloat16 [32, 512, 5120], P('section', 'dp'), may hold values from -45 to 45
- x_bwd: bfloat16 [32, 512, 5120], P('section', 'dp'), may hold values from -45 to 45
- grad_in: bfloat16 [32, 512, 5120], P('section', 'dp'), may hold values from -25 to 25
- gain: float32 [32, 5120], P('section'), may hold values from 0.1 to 1.9
- weight: bfloat16 [32, 5120, 3072], P('section', 'dp'), may hold values from -0.078125 to 0.078125
- damping: float32 [32], P('section'), may hold values from 0.1 to 1
Outputs:
- next_fwd: bfloat16 [32, 512, 5120], P('section', 'dp')
- next_grad: bfloat16 [32, 512, 5120], P('section', 'dp')
- update: bfloat16 [32, 5120, 3072], P('section', 'dp')
The draws below stay inside these ranges and needn't reach their ends.
All inputs are finite; a program needn't handle non-finite values.
Results may differ from the reference program's by a relative error of at most 0.012.
The reference program's roundings to bfloat16 on the way count: a program that leaves them out, or rounds other values in their place, can miss the bound.
Values may be sent and summed in bfloat16 or wider, within the bound.
No kernel may reach another device: no remote copies, remote signals or barrier semaphores. Data moves between devices by JAX's collectives and lax.ppermute only.
A program may use at most 128 MiB of HBM per device.

```python
import math
import jax
import jax.numpy as jnp
from jax import lax

D = 5120
DW = 3072
BLOCK = 1024
TOK_DEV = 64
SECTIONS = 32
TOKG = 512
WROWS = 640
NBLK_A = 5
NBLK_G = 3


def spread_scales(key, base, low, high):
    row_key, col_key = jax.random.split(key)
    row_scale = jnp.exp(jax.random.uniform(row_key, (base.shape[0], base.shape[1], 1), jnp.float32, math.log(low), math.log(high)))
    col_scale = jnp.exp(jax.random.uniform(col_key, (base.shape[0], 1, base.shape[2]), jnp.float32, math.log(low), math.log(high)))
    return base * row_scale * col_scale


def shared_tokens(key):
    factor_rank = max(1, min(32, TOKG // 8))
    return jax.random.normal(jax.random.fold_in(key, 101), (SECTIONS, TOKG, factor_rank), jnp.float32)


def mix_tokens(common, loading):
    product = jnp.einsum('str,srd->std', common, loading, precision=lax.Precision.HIGHEST)
    return product / math.sqrt(common.shape[2])


def draw_x_fwd(key, part):
    key = jax.random.fold_in(key, 11)
    base_key, scale_key = jax.random.split(key)
    base = jnp.clip(jax.random.normal(base_key, (SECTIONS, TOKG, D), jnp.float32), -4.0, 4.0)
    return spread_scales(scale_key, base, 0.3, 3.0).astype(jnp.bfloat16)


def draw_x_bwd(key, part):
    common = shared_tokens(key)
    key = jax.random.fold_in(key, 13)
    load_key, noise_key, scale_key = jax.random.split(key, 3)
    loading = jax.random.normal(load_key, (SECTIONS, common.shape[2], D), jnp.float32)
    noise = jnp.clip(jax.random.normal(noise_key, (SECTIONS, TOKG, D), jnp.float32), -4.0, 4.0)
    base = jnp.clip(mix_tokens(common, loading) + 0.3 * noise, -4.0, 4.0)
    return spread_scales(scale_key, base, 0.3, 3.0).astype(jnp.bfloat16)


def draw_grad_in(key, part):
    common = shared_tokens(key)
    key = jax.random.fold_in(key, 23)
    load_key, noise_key, row_key, group_key = jax.random.split(key, 4)
    position = jnp.arange(SECTIONS, dtype=jnp.float32)[:, None, None] / max(SECTIONS - 1, 1)
    row_scale = jnp.exp(jax.random.uniform(row_key, (SECTIONS, TOKG // TOK_DEV, TOK_DEV, 1), jnp.float32, math.log(0.7), math.log(1.4)))
    group_scale = jnp.exp(jax.random.uniform(group_key, (SECTIONS, TOKG // TOK_DEV, 1, 1), jnp.float32, math.log(0.5), math.log(2.0)))
    token_scale = (row_scale * group_scale).reshape(SECTIONS, TOKG, 1)
    loading = jax.random.normal(load_key, (SECTIONS, common.shape[2], D), jnp.float32)
    noise = jnp.clip(jax.random.normal(noise_key, (SECTIONS, TOKG, D), jnp.float32), -4.0, 4.0)
    base = jnp.clip(mix_tokens(common, loading) + 0.3 * noise, -2.9, 2.9)
    level = 0.1 * 30.0 ** position
    return (base * token_scale * level).astype(jnp.bfloat16)


def levels(key, extent, shards, low, largest):
    level = 1.0
    for dim, parts in shards:
        steps = jax.random.uniform(jax.random.fold_in(jax.random.fold_in(key, 6), dim), (parts,), jnp.float32, low / len(shards), largest / len(shards))
        level = level * jnp.repeat(jnp.exp(steps), extent[dim] // parts).reshape((-1,) + (1,) * (len(extent) - 1 - dim))
    return level


def centred(own_key, dims, width, most, shards=(), kind=jnp.bfloat16):
    values = jax.random.normal(own_key, dims, jnp.float32) * width
    if len(shards) > 0:
        values = levels(own_key, dims, shards, -0.22, 0.18) * values
    return jnp.clip(values, min=-most, max=most).astype(kind)


def setup_inputs(seed: int = 0) -> dict:
    splits = jax.random.split(jax.random.key(seed), 7)
    return {
        "x_fwd": draw_x_fwd(jax.random.fold_in(splits[6], 71), 0),
        "x_bwd": draw_x_bwd(jax.random.fold_in(splits[6], 71), 0),
        "grad_in": draw_grad_in(jax.random.fold_in(splits[6], 71), 0),
        "gain": jnp.clip(1.0 + 0.18 * jax.random.normal(splits[3], (SECTIONS, D), jnp.float32), 0.1, 1.9),
        "weight": centred(splits[4], (SECTIONS, D, DW), D ** -0.5, 0.078125, ((0, 32), (1, 8))),
        "damping": jnp.clip(jnp.exp(math.log(1.0) - 2.3025851 * jax.random.uniform(splits[5], (SECTIONS,), jnp.float32) ** levels(splits[5], (SECTIONS,), ((0, 32),), -0.2, 0.2)), 0.1, 1.0),
    }


EPS = 1e-06

def normalize(x, gain):
    wide = x.astype(jnp.float32)
    scale = lax.rsqrt(lax.optimization_barrier(jnp.mean(wide * wide, axis=-1, keepdims=True)) + EPS)
    return ((wide * scale * gain).astype(jnp.bfloat16), scale)

def precondition(rows, damping):
    gram = jnp.dot(rows.T.astype(jnp.float32), rows.astype(jnp.float32), preferred_element_type=jnp.float32) / TOKG
    factor = gram + damping * jnp.eye(BLOCK, dtype=jnp.float32)
    lower = jnp.linalg.cholesky(factor)
    first = jax.scipy.linalg.solve_triangular(lower, rows.T.astype(jnp.float32), lower=True)
    second = jax.scipy.linalg.solve_triangular(lower, first, lower=True, trans=1)
    return second.T.astype(jnp.bfloat16)

def one_section(inputs):
    fwd, bwd, grad, gain, weight, damping = inputs
    gain_wide = gain.astype(jnp.float32)
    normed_f, _ = normalize(fwd, gain_wide)
    grouped = normed_f.astype(jnp.float32).reshape(TOKG, D // WROWS, WROWS)
    weight_groups = weight.astype(jnp.float32).reshape(D // WROWS, WROWS, DW)
    partials = jnp.einsum('tgk,gkw->gtw', grouped, weight_groups)
    partials = lax.optimization_barrier(partials.astype(jnp.bfloat16))
    layer_out = lax.optimization_barrier(jnp.sum(partials.astype(jnp.float32), axis=0))
    wide_f = fwd.astype(jnp.float32)
    out_f = jnp.concatenate([wide_f[:, :DW] + layer_out, wide_f[:, DW:]], axis=1).astype(jnp.bfloat16)
    normed_b, scale_b = normalize(bwd, gain_wide)
    upstream = grad[:, :DW]
    back_n = lax.dot_general(upstream.astype(jnp.float32), weight.astype(jnp.float32), (((1,), (1,)), ((), ())), preferred_element_type=jnp.float32)
    back_n = lax.optimization_barrier(back_n.astype(jnp.bfloat16))
    wide_b = bwd.astype(jnp.float32)
    scaled = back_n.astype(jnp.float32) * gain_wide
    inner = lax.optimization_barrier(jnp.mean(scaled * wide_b, axis=-1, keepdims=True))
    back_x = grad.astype(jnp.float32) + scale_b * scaled - wide_b * scale_b ** 3 * inner
    out_b = back_x.astype(jnp.bfloat16)
    blocks = jnp.concatenate([normed_b.reshape(TOKG, NBLK_A, BLOCK), upstream.reshape(TOKG, NBLK_G, BLOCK)], axis=1)
    solved = lax.map(lambda rows: precondition(rows, damping), jnp.transpose(blocks, (1, 0, 2)))
    solved = jnp.transpose(solved, (1, 0, 2))
    act_tilde = solved[:, :NBLK_A].reshape(TOKG, D)
    grad_tilde = solved[:, NBLK_A:].reshape(TOKG, DW)
    left = jnp.dot(act_tilde.astype(jnp.float32), normed_b.T.astype(jnp.float32), preferred_element_type=jnp.float32)
    right = jnp.dot(grad_tilde.astype(jnp.float32), upstream.T.astype(jnp.float32), preferred_element_type=jnp.float32)
    term = jnp.sum(left * right)
    return (out_f, out_b, act_tilde, grad_tilde, term)

def reference(x_fwd, x_bwd, grad_in, gain, weight, damping):
    out_f, out_b, act_tilde, grad_tilde, terms = lax.map(one_section, (x_fwd, x_bwd, grad_in, gain, weight, damping))
    total = jnp.sum(terms)
    ratio = jnp.sqrt(jnp.float32(SECTIONS * D * DW) / total)

    def finish(pair):
        product = jnp.dot(pair[0].T.astype(jnp.float32), pair[1].astype(jnp.float32), preferred_element_type=jnp.float32)
        return (ratio * product).astype(jnp.bfloat16)
    update = lax.map(finish, (act_tilde, grad_tilde))
    next_fwd = jnp.concatenate([jnp.zeros_like(out_f[:1]), out_f[:-1]], axis=0)
    next_grad = jnp.concatenate([out_b[1:], jnp.zeros_like(out_b[:1])], axis=0)
    return (next_fwd, next_grad, update)
```

```python
import jax
import jax.numpy as jnp
from jax import lax
from jax.experimental import pallas as pl
from jax.experimental.pallas import tpu as pltpu
from jax.sharding import PartitionSpec as P

BLOCK = 1024
EPS = 1e-06
F32 = jnp.float32
BF16 = jnp.bfloat16
EXACT = lax.Precision.HIGHEST


def dot(a, b, contract=(1, 0), precision=EXACT):
    return lax.dot_general(
        a,
        b,
        (((contract[0],), (contract[1],)), ((), ())),
        precision=precision,
        preferred_element_type=F32,
    )


def from_behind(value, axis, steps):
    count = lax.axis_size(axis)
    leading, last = (max(0, -steps), min(count, count - steps))
    return lax.ppermute(value, axis, [(source, source + steps) for source in range(leading, last)])


def normalize(x, gain):
    wide = x.astype(F32)
    scale = lax.rsqrt(jnp.mean(wide * wide, axis=-1, keepdims=True) + EPS)
    return ((wide * scale * gain).astype(BF16), scale)


def eye_mask(order):
    rows = lax.broadcasted_iota(jnp.int32, (order, order), 0)
    return rows == lax.broadcasted_iota(jnp.int32, (order, order), 1)


def step_coefficients(low, high):
    mid, half = (low + high) * 0.5, (high - low) * 0.5
    scale = 1.0 / (2.0 * mid * mid - half * half)
    return 4.0 * mid * scale, 2.0 * scale, half * half * scale


def invert(matrices, low, state):
    order = matrices[0].shape[0]
    eye = eye_mask(order).astype(F32)
    spreads = []
    for index, matrix in enumerate(matrices):
        inverse_bound = 1.0 / jnp.max(jnp.sum(jnp.abs(matrix), axis=1, keepdims=True))
        first, second, spread = step_coefficients(low * inverse_bound, jnp.float32(1.0))
        scaled = matrix * inverse_bound
        state[index, :order] = inverse_bound * (first * eye - second * scaled)
        state[index, order:] = first * scaled - second * dot(scaled, scaled)
        spreads.append(spread)

    def unfinished(spreads):
        worst = spreads[0]
        for spread in spreads[1:]:
            worst = jnp.maximum(worst, spread)
        return worst > 2e-3

    def step(spreads):
        later = []
        for index, spread in enumerate(spreads):
            first, second, after = step_coefficients(1.0 - spread, 1.0 + spread)
            both = state[index]
            state[index] = first * both - second * dot(both, both[order:])
            later.append(after)
        return tuple(later)

    lax.while_loop(unfinished, step, tuple(spreads))
    result = []
    for index, matrix in enumerate(matrices):
        guess = state[index, :order]
        result.append(2.0 * guess - dot(guess, dot(matrix, guess)))
    return result


def split(value):
    high = value.astype(BF16)
    rest = value - high.astype(F32)
    middle = rest.astype(BF16)
    return high, middle, (rest - middle.astype(F32)).astype(BF16)


def apply_inverse(rows_list, damping, factor, state, store):
    count = rows_list[0].shape[0]
    half = count // 2
    eye = eye_mask(count)
    for index, rows in enumerate(rows_list):
        gram = dot(rows, rows, (1, 1), None) * (1.0 / count)
        factor[index] = jnp.where(eye, gram + damping, gram)
    every = range(len(rows_list))
    corner = invert([factor[i, :half, :half] for i in every], damping, state)
    upper = [factor[i, :half, half:] for i in every]
    tall = [dot(corner[i], upper[i]) for i in every]
    rest = [factor[i, half:, half:] - dot(upper[i], tall[i], (0, 0)) for i in every]
    rest = invert(rest, damping, state)
    cross = [dot(tall[i], rest[i]) for i in every]
    for i, rows in enumerate(rows_list):
        factor[i, :half, :half] = corner[i] + dot(cross[i], tall[i], (1, 1))
        factor[i, :half, half:] = -cross[i]
        factor[i, half:, :half] = -cross[i].T
        factor[i, half:, half:] = rest[i]
        high, middle, low = split(factor[i])
        solved = dot(low, rows, precision=None) + dot(middle, rows, precision=None)
        store(i, (solved + dot(high, rows, precision=None)).astype(BF16))


def act_kernel(damping_ref, rows_ref, solved_ref, left_ref, factor, state):
    def store(_, solved):
        solved_ref[...] = solved

    apply_inverse([rows_ref[...]], damping_ref[0, 0], factor, state, store)
    left_ref[...] = dot(solved_ref[...], rows_ref[...], (1, 1), None)


def grad_kernel(damping_ref, rows_ref, left_ref, solved_ref, term_ref, factor, state):
    blocks = rows_ref.shape[1] // BLOCK

    def store(index, solved):
        solved_ref[:, index * BLOCK : (index + 1) * BLOCK] = solved

    rows = [rows_ref[:, i * BLOCK : (i + 1) * BLOCK] for i in range(blocks)]
    apply_inverse(rows, damping_ref[0, 0], factor, state, store)
    right = dot(solved_ref[...], rows_ref[...], (1, 1), None)
    product = jnp.sum(left_ref[...] * right, axis=0, keepdims=True)
    term_ref[...] = jnp.sum(product, axis=1, keepdims=True)


VMEM = pl.BlockSpec(memory_space=pltpu.VMEM)
SMEM = pl.BlockSpec(memory_space=pltpu.SMEM)


def solve_act(damping, rows):
    count, width = rows.shape
    return pl.pallas_call(
        act_kernel,
        out_shape=(
            jax.ShapeDtypeStruct((count, width), BF16),
            jax.ShapeDtypeStruct((count, count), F32),
        ),
        in_specs=[SMEM, VMEM],
        out_specs=(VMEM, VMEM),
        scratch_shapes=[
            pltpu.VMEM((1, count, count), F32),
            pltpu.VMEM((1, count, count // 2), F32),
        ],
        compiler_params=pltpu.CompilerParams(vmem_limit_bytes=40 * 2**20),
        cost_estimate=pl.CostEstimate(
            flops=16 * 10**9, bytes_accessed=4 * 2**20, transcendentals=0
        ),
        name="solve_act",
    )(damping, rows)


def solve_grad(damping, rows, left):
    count, width = rows.shape
    blocks = width // BLOCK
    return pl.pallas_call(
        grad_kernel,
        out_shape=(
            jax.ShapeDtypeStruct((count, width), BF16),
            jax.ShapeDtypeStruct((1, 1), F32),
        ),
        in_specs=[SMEM, VMEM, VMEM],
        out_specs=(VMEM, VMEM),
        scratch_shapes=[
            pltpu.VMEM((blocks, count, count), F32),
            pltpu.VMEM((blocks, count, count // 2), F32),
        ],
        compiler_params=pltpu.CompilerParams(vmem_limit_bytes=48 * 2**20),
        cost_estimate=pl.CostEstimate(
            flops=45 * 10**9, bytes_accessed=8 * 2**20, transcendentals=0
        ),
        name="solve_grad",
    )(damping, rows, left)


def per_device(x_fwd, x_bwd, grad_in, gain, weight, damping):
    fwd = x_fwd[0]
    bwd = x_bwd[0]
    grad = grad_in[0]
    gain_wide = gain[0]
    local_w = weight[0]
    tokens, width = fwd.shape
    own_rows, out_width = local_w.shape
    groups = lax.axis_size("dp")
    act_blocks = width // BLOCK
    damp_value = damping.reshape(1, 1)

    upstream = grad[:, :out_width]
    group_grad = lax.all_gather(upstream, "dp", axis=0, tiled=True)

    normed_b, scale_b = normalize(bwd, gain_wide)
    blocks = jnp.pad(
        jnp.moveaxis(normed_b.reshape(tokens, act_blocks, BLOCK), 1, 0),
        ((0, groups - act_blocks), (0, 0), (0, 0)),
    )
    block_rows = lax.all_to_all(blocks, "dp", 0, 0, tiled=True).reshape(groups * tokens, BLOCK)
    normed_f, _ = normalize(fwd, gain_wide)
    rows_f = lax.all_to_all(normed_f, "dp", split_axis=1, concat_axis=0, tiled=True)

    solved, left = solve_act(damp_value, block_rows)
    solved = solved.reshape(groups, tokens, BLOCK)
    own_solved = lax.all_to_all(solved, "dp", 0, 0, tiled=True)[:act_blocks]
    act_tilde = jnp.moveaxis(own_solved, 0, 1).reshape(tokens, width)
    act_rows = lax.all_to_all(act_tilde, "dp", split_axis=1, concat_axis=0, tiled=True)

    partial = jnp.dot(rows_f, local_w, preferred_element_type=F32).astype(BF16)
    partials = lax.all_to_all(
        partial.reshape(groups, tokens, out_width), "dp", 0, 0, tiled=True
    )
    layer_out = jnp.sum(partials.astype(F32), axis=0)
    wide_f = fwd.astype(F32)
    out_f = jnp.concatenate(
        [wide_f[:, :out_width] + layer_out, wide_f[:, out_width:]], axis=1
    ).astype(BF16)
    next_fwd = from_behind(out_f, "section", 1)

    back_rows = lax.dot_general(
        group_grad, local_w, (((1,), (1,)), ((), ())), preferred_element_type=F32
    ).astype(BF16)
    back_n = lax.all_to_all(back_rows, "dp", split_axis=0, concat_axis=1, tiled=True)
    wide_b = bwd.astype(F32)
    scaled = back_n.astype(F32) * gain_wide
    inner = jnp.mean(scaled * wide_b, axis=-1, keepdims=True)
    out_b = (grad.astype(F32) + scale_b * scaled - wide_b * scale_b**3 * inner).astype(BF16)
    next_grad = from_behind(out_b, "section", -1)

    grad_tilde, term = solve_grad(damp_value, group_grad, left)
    devices = lax.axis_size("section") * groups
    spread = jnp.broadcast_to(term, (devices, 128))
    terms = lax.all_to_all(spread, ("section", "dp"), 0, 0, tiled=True)
    total = jnp.sum(terms[:, 0])
    precond = lax.dot_general(
        act_rows, grad_tilde, (((0,), (0,)), ((), ())), preferred_element_type=F32
    )
    entries = lax.axis_size("section") * width * out_width
    ratio = jnp.sqrt(jnp.float32(entries) / total)
    update = (ratio * precond).astype(BF16)
    return (next_fwd[None], next_grad[None], update[None])


def solution(mesh):
    return jax.shard_map(
        per_device,
        mesh=mesh,
        in_specs=(
            P("section", "dp", None),
            P("section", "dp", None),
            P("section", "dp", None),
            P("section", None),
            P("section", "dp", None),
            P("section"),
        ),
        out_specs=(P("section", "dp", None), P("section", "dp", None), P("section", "dp", None)),
        check_vma=False,
    )
```

```python
import jax
import jax.numpy as jnp
from jax import lax
from jax.experimental import pallas as pl
from jax.experimental.pallas import tpu as pltpu
from jax.sharding import PartitionSpec as P

BLOCK = 1024
EPS = 1e-06
F32 = jnp.float32
BF16 = jnp.bfloat16
EXACT = lax.Precision.HIGHEST


def dot(a, b, contract=(1, 0), precision=EXACT):
    return lax.dot_general(
        a,
        b,
        (((contract[0],), (contract[1],)), ((), ())),
        precision=precision,
        preferred_element_type=F32,
    )


def from_behind(value, axis, steps):
    count = lax.axis_size(axis)
    leading, last = (max(0, -steps), min(count, count - steps))
    return lax.ppermute(value, axis, [(source, source + steps) for source in range(leading, last)])


def normalize(x, gain):
    wide = x.astype(F32)
    scale = lax.rsqrt(jnp.mean(wide * wide, axis=-1, keepdims=True) + EPS)
    return ((wide * scale * gain).astype(BF16), scale)


def eye_mask(order):
    rows = lax.broadcasted_iota(jnp.int32, (order, order), 0)
    return rows == lax.broadcasted_iota(jnp.int32, (order, order), 1)


def step_coefficients(low, high):
    mid, half = (low + high) * 0.5, (high - low) * 0.5
    scale = 1.0 / (2.0 * mid * mid - half * half)
    return 4.0 * mid * scale, 2.0 * scale, half * half * scale


def invert(matrices, low, state):
    order = matrices[0].shape[0]
    eye = eye_mask(order).astype(F32)
    spreads = []
    for index, matrix in enumerate(matrices):
        inverse_bound = 1.0 / jnp.max(jnp.sum(jnp.abs(matrix), axis=1, keepdims=True))
        first, second, spread = step_coefficients(low * inverse_bound, jnp.float32(1.0))
        scaled = matrix * inverse_bound
        state[index, :order] = inverse_bound * (first * eye - second * scaled)
        state[index, order:] = first * scaled - second * dot(scaled, scaled)
        spreads.append(spread)

    def unfinished(spreads):
        worst = spreads[0]
        for spread in spreads[1:]:
            worst = jnp.maximum(worst, spread)
        return worst > 2e-3

    def step(spreads):
        later = []
        for index, spread in enumerate(spreads):
            first, second, after = step_coefficients(1.0 - spread, 1.0 + spread)
            both = state[index]
            state[index] = first * both - second * dot(both, both[order:])
            later.append(after)
        return tuple(later)

    lax.while_loop(unfinished, step, tuple(spreads))
    result = []
    for index, matrix in enumerate(matrices):
        guess = state[index, :order]
        result.append(2.0 * guess - dot(guess, dot(matrix, guess)))
    return result


def split(value):
    high = value.astype(BF16)
    rest = value - high.astype(F32)
    middle = rest.astype(BF16)
    return high, middle, (rest - middle.astype(F32)).astype(BF16)


def apply_inverse(rows_list, damping, factor, state, store):
    count = rows_list[0].shape[0]
    half = count // 2
    eye = eye_mask(count)
    for index, rows in enumerate(rows_list):
        gram = dot(rows, rows, (1, 1), None) * (1.0 / count)
        factor[index] = jnp.where(eye, gram + damping, gram)
    every = range(len(rows_list))
    corner = invert([factor[i, :half, :half] for i in every], damping, state)
    upper = [factor[i, :half, half:] for i in every]
    tall = [dot(corner[i], upper[i]) for i in every]
    rest = [factor[i, half:, half:] - dot(upper[i], tall[i], (0, 0)) for i in every]
    rest = invert(rest, damping, state)
    cross = [dot(tall[i], rest[i]) for i in every]
    for i, rows in enumerate(rows_list):
        factor[i, :half, :half] = corner[i] + dot(cross[i], tall[i], (1, 1))
        factor[i, :half, half:] = -cross[i]
        factor[i, half:, :half] = -cross[i].T
        factor[i, half:, half:] = rest[i]
        high, middle, low = split(factor[i])
        solved = dot(low, rows, precision=None) + dot(middle, rows, precision=None)
        store(i, (solved + dot(high, rows, precision=None)).astype(BF16))


def act_kernel(damping_ref, rows_ref, solved_ref, left_ref, factor, state):
    def store(_, solved):
        solved_ref[...] = solved

    rows = rows_ref[:, :BLOCK]
    apply_inverse([rows], damping_ref[0, 0], factor, state, store)
    left_ref[...] = dot(solved_ref[...], rows, (1, 1), None)


def grad_kernel(damping_ref, rows_ref, left_ref, solved_ref, term_ref, factor, state):
    blocks = rows_ref.shape[1] // BLOCK

    def store(index, solved):
        solved_ref[:, index * BLOCK : (index + 1) * BLOCK] = solved

    rows = [rows_ref[:, i * BLOCK : (i + 1) * BLOCK] for i in range(blocks)]
    apply_inverse(rows, damping_ref[0, 0], factor, state, store)
    right = dot(solved_ref[...], rows_ref[...], (1, 1), None)
    product = jnp.sum(left_ref[...] * right, axis=0, keepdims=True)
    term_ref[...] = jnp.sum(product, axis=1, keepdims=True)


VMEM = pl.BlockSpec(memory_space=pltpu.VMEM)
SMEM = pl.BlockSpec(memory_space=pltpu.SMEM)


def solve_act(damping, rows):
    count = rows.shape[0]
    return pl.pallas_call(
        act_kernel,
        out_shape=(
            jax.ShapeDtypeStruct((count, BLOCK), BF16),
            jax.ShapeDtypeStruct((count, count), F32),
        ),
        in_specs=[SMEM, VMEM],
        out_specs=(VMEM, VMEM),
        scratch_shapes=[
            pltpu.VMEM((1, count, count), F32),
            pltpu.VMEM((1, count, count // 2), F32),
        ],
        compiler_params=pltpu.CompilerParams(vmem_limit_bytes=40 * 2**20),
        cost_estimate=pl.CostEstimate(
            flops=16 * 10**9, bytes_accessed=4 * 2**20, transcendentals=0
        ),
        name="solve_act",
    )(damping, rows)


def solve_grad(damping, rows, left):
    count, width = rows.shape
    blocks = width // BLOCK
    return pl.pallas_call(
        grad_kernel,
        out_shape=(
            jax.ShapeDtypeStruct((count, width), BF16),
            jax.ShapeDtypeStruct((1, 1), F32),
        ),
        in_specs=[SMEM, VMEM, VMEM],
        out_specs=(VMEM, VMEM),
        scratch_shapes=[
            pltpu.VMEM((blocks, count, count), F32),
            pltpu.VMEM((blocks, count, count // 2), F32),
        ],
        compiler_params=pltpu.CompilerParams(vmem_limit_bytes=48 * 2**20),
        cost_estimate=pl.CostEstimate(
            flops=45 * 10**9, bytes_accessed=8 * 2**20, transcendentals=0
        ),
        name="solve_grad",
    )(damping, rows, left)


OWNERS = (0, 2, 4, 5, 7)
UNIT = 128
HOPS = (
    (((0, 1), (4, 3), (7, 6)), {0: 4, 4: 0, 7: 0}, 4, {1: -1, 3: 1, 6: 2}),
    (((2, 1), (5, 6)), {2: 0, 5: 6}, 2, {1: 3, 6: 0}),
    (((2, 3), (5, 4)), {2: 7, 5: 0}, 1, {3: 0, 4: 4}),
)
KEPT = ({0: 0, 2: 2, 4: 3, 5: 1, 7: 3}, 5, {0: 0, 2: 0, 4: -1, 5: 0, 7: 0})


def lookup(table, missing, me):
    return jnp.array([table.get(i, missing) for i in range(8)], jnp.int32)[me]


def spread_act(solved, me):
    count = solved.shape[0]
    window, dump = 5, 7
    buffer = jnp.zeros((count, (dump + window) * UNIT), solved.dtype)

    def place(buffer, piece, table):
        offset = jnp.where(
            lookup(table, 99, me) == 99, dump, lookup(table, 99, me) + 1
        )
        return lax.dynamic_update_slice(buffer, piece, (0, offset * UNIT))

    first, units, table = KEPT
    piece = lax.dynamic_slice_in_dim(solved, lookup(first, 0, me) * UNIT, units * UNIT, 1)
    buffer = place(buffer, piece, table)
    for pairs, first, units, table in HOPS:
        piece = lax.dynamic_slice_in_dim(solved, lookup(first, 0, me) * UNIT, units * UNIT, 1)
        buffer = place(buffer, lax.ppermute(piece, "dp", pairs), table)
    return buffer[:, UNIT : (window + 1) * UNIT]


def swap(value, offset):
    return lax.ppermute(value, "dp", [(i, i ^ offset) for i in range(8)])


def gather_pieces(value):
    half = value.shape[0] // 2
    other = swap(value, 4)
    direct = [swap(value, 1), swap(value, 3), swap(other, 1), swap(other, 3)]
    pieces, places = [value, other] + direct, [(0, 0), (4, 0), (1, 0), (3, 0), (5, 0), (7, 0)]
    for near, far, offset in ((direct[0], direct[1], 2), (direct[2], direct[3], 6)):
        pieces += [swap(far[:half], 1), swap(near[half:], 3)]
        places += [(offset, 0), (offset, half)]
    return pieces, places, direct


def normalize_kernel(fwd_ref, bwd_ref, gain_ref, out_ref):
    gain = gain_ref[...]
    normed_b, _ = normalize(bwd_ref[...], gain)
    normed_f, _ = normalize(fwd_ref[...], gain)
    part = normed_f.shape[1] // out_ref.shape[0]
    for device in range(out_ref.shape[0]):
        if device in OWNERS:
            block = OWNERS.index(device)
            out_ref[device, :, :BLOCK] = normed_b[:, block * BLOCK : (block + 1) * BLOCK]
        else:
            out_ref[device, :, :BLOCK] = jnp.zeros((normed_b.shape[0], BLOCK), BF16)
        out_ref[device, :, BLOCK:] = normed_f[:, device * part : (device + 1) * part]


def forward_kernel(rows_ref, weight_ref, out_ref):
    out_ref[...] = dot(rows_ref[:, BLOCK:], weight_ref[...], precision=None).astype(BF16)


def backward_kernel(places, me_ref, *refs):
    me = me_ref[0, 0]
    pieces, (weight_ref, gathered, *outs), scratch = (
        refs[: len(places)],
        refs[len(places) : -1],
        refs[-1],
    )
    tokens = outs[0].shape[0]
    for piece, (offset, first) in zip(pieces, places):
        start = pl.multiple_of((me ^ offset) * tokens + first, 32)
        gathered[pl.ds(start, piece.shape[0]), :] = piece[...]
    scratch[...] = dot(gathered[...], weight_ref[...], (1, 1), None).astype(BF16)
    for offset, out in enumerate(outs):
        start = pl.multiple_of((me ^ offset) * tokens, tokens)
        out[...] = scratch[pl.ds(start, tokens), :]


def finish_backward_kernel(me_ref, *refs):
    me = me_ref[0, 0]
    pieces, (bwd_ref, grad_ref, gain_ref, out_ref, back) = refs[:8], refs[8:]
    part = pieces[0].shape[1]
    for offset, piece in enumerate(pieces):
        start = pl.multiple_of((me ^ offset) * part, UNIT)
        back[:, pl.ds(start, part)] = piece[...]
    wide = bwd_ref[...].astype(F32)
    scale = lax.rsqrt(jnp.mean(wide * wide, axis=-1, keepdims=True) + EPS)
    scaled = back[...].astype(F32) * gain_ref[...]
    inner = jnp.mean(scaled * wide, axis=-1, keepdims=True)
    out = grad_ref[...].astype(F32) + scale * scaled - wide * scale**3 * inner
    out_ref[...] = out.astype(BF16)


def update_kernel(entries, terms_ref, act_ref, grad_ref, out_ref, turned):
    @pl.when(pl.program_id(0) == 0)
    def _():
        turned[...] = act_ref[...].T

    terms = terms_ref[...]
    total = jnp.sum(jnp.sum(terms, axis=0, keepdims=True)[:, :1], axis=1, keepdims=True)
    ratio = jnp.sqrt(entries / total)
    out_ref[...] = (ratio * dot(turned[...], grad_ref[...], precision=None)).astype(BF16)


def shape(*dims, dtype=BF16):
    return jax.ShapeDtypeStruct(dims, dtype)


def cost(flops, moved):
    return pl.CostEstimate(flops=flops, bytes_accessed=moved, transcendentals=0)


def params(mib):
    return pltpu.CompilerParams(vmem_limit_bytes=mib * 2**20)


def per_device(x_fwd, x_bwd, grad_in, gain, weight, damping):
    fwd = x_fwd[0]
    bwd = x_bwd[0]
    grad = grad_in[0]
    local_w = weight[0]
    tokens, width = fwd.shape
    own_rows, out_width = local_w.shape
    groups = lax.axis_size("dp")
    group = groups * tokens
    me = lax.axis_index("dp")
    me_value = me.reshape(1, 1)
    damp_value = damping.reshape(1, 1)

    pieces, places, direct = gather_pieces(grad[:, :out_width])

    sent = pl.pallas_call(
        normalize_kernel,
        out_shape=shape(groups, tokens, BLOCK + own_rows),
        in_specs=[VMEM] * 3,
        out_specs=VMEM,
        compiler_params=params(32),
        cost_estimate=cost(10**7, 3 * 10**6),
        name="normalize",
    )(fwd, bwd, gain)
    rows = lax.all_to_all(sent, "dp", 0, 0, tiled=True).reshape(group, BLOCK + own_rows)

    columns = 512
    partial = pl.pallas_call(
        forward_kernel,
        grid=(out_width // columns,),
        out_shape=shape(group, out_width),
        in_specs=[
            pl.BlockSpec((group, BLOCK + own_rows), lambda i: (0, 0)),
            pl.BlockSpec((own_rows, columns), lambda i: (0, i)),
        ],
        out_specs=pl.BlockSpec((group, columns), lambda i: (0, i)),
        compiler_params=params(32),
        cost_estimate=cost(2 * 10**9, 8 * 10**6),
        name="forward",
    )(rows, local_w)
    partials = lax.all_to_all(
        partial.reshape(groups, tokens, out_width), "dp", 0, 0, tiled=True
    )

    rows_late, *_ = lax.optimization_barrier((rows, partial, *direct))
    solved, left = solve_act(damp_value, rows_late)
    act_rows = spread_act(solved, me)

    ready = lax.optimization_barrier((me_value, *pieces, solved))
    group_grad, *back_rows = pl.pallas_call(
        lambda *refs: backward_kernel(places, *refs),
        out_shape=(shape(group, out_width),) + (shape(tokens, own_rows),) * groups,
        in_specs=[SMEM] + [VMEM] * (len(pieces) + 1),
        out_specs=(VMEM,) * (groups + 1),
        scratch_shapes=[pltpu.VMEM((group, own_rows), BF16)],
        compiler_params=params(40),
        cost_estimate=cost(2 * 10**9, 10**7),
        name="backward",
    )(*ready[:-1], local_w)
    back = [back_rows[0]] + [swap(back_rows[k], k) for k in range(1, groups)]

    group_grad, act_rows = lax.optimization_barrier((group_grad, act_rows))
    grad_tilde, term = solve_grad(damp_value, group_grad, left)

    term, partials, *back = lax.optimization_barrier((term, partials, *back))
    devices = lax.axis_size("section") * groups
    terms = lax.all_to_all(
        jnp.broadcast_to(term, (devices, 128)), ("section", "dp"), 0, 0, tiled=True
    )

    layer_out = jnp.sum(partials.astype(F32), axis=0)
    wide_f = fwd.astype(F32)
    out_f = jnp.concatenate(
        [wide_f[:, :out_width] + layer_out, wide_f[:, out_width:]], axis=1
    ).astype(BF16)
    next_fwd = from_behind(out_f, "section", 1)

    out_b = pl.pallas_call(
        finish_backward_kernel,
        out_shape=shape(tokens, width),
        in_specs=[SMEM] + [VMEM] * (groups + 3),
        out_specs=VMEM,
        scratch_shapes=[pltpu.VMEM((tokens, width), BF16)],
        compiler_params=params(32),
        cost_estimate=cost(10**7, 3 * 10**6),
        name="finish_backward",
    )(me_value, *back, bwd, grad, gain)
    next_grad = from_behind(out_b, "section", -1)

    entries = float(lax.axis_size("section") * width * out_width)
    update = pl.pallas_call(
        lambda *refs: update_kernel(entries, *refs),
        grid=(out_width // columns,),
        out_shape=shape(own_rows, out_width),
        in_specs=[
            pl.BlockSpec((devices, 128), lambda i: (0, 0)),
            pl.BlockSpec((group, own_rows), lambda i: (0, 0)),
            pl.BlockSpec((group, columns), lambda i: (0, i)),
        ],
        out_specs=pl.BlockSpec((own_rows, columns), lambda i: (0, i)),
        scratch_shapes=[pltpu.VMEM((own_rows, group), BF16)],
        compiler_params=params(32),
        cost_estimate=cost(2 * 10**9, 8 * 10**6),
        name="update",
    )(terms, act_rows, grad_tilde)
    return (next_fwd[None], next_grad[None], update[None])


def solution(mesh):
    return jax.shard_map(
        per_device,
        mesh=mesh,
        in_specs=(
            P("section", "dp", None),
            P("section", "dp", None),
            P("section", "dp", None),
            P("section", None),
            P("section", "dp", None),
            P("section"),
        ),
        out_specs=(P("section", "dp", None), P("section", "dp", None), P("section", "dp", None)),
        check_vma=False,
    )
```

```python
import jax
import jax.numpy as jnp
from jax import lax
from jax.experimental import pallas as pl
from jax.experimental.pallas import tpu as pltpu
from jax.sharding import PartitionSpec as P

BLOCK = 1024
EPS = 1e-06
F32 = jnp.float32
BF16 = jnp.bfloat16
EXACT = lax.Precision.HIGHEST


def dot(a, b, contract=(1, 0), precision=EXACT):
    return lax.dot_general(
        a,
        b,
        (((contract[0],), (contract[1],)), ((), ())),
        precision=precision,
        preferred_element_type=F32,
    )


def from_behind(value, axis, steps):
    count = lax.axis_size(axis)
    leading, last = (max(0, -steps), min(count, count - steps))
    return lax.ppermute(value, axis, [(source, source + steps) for source in range(leading, last)])


def normalize(x, gain):
    wide = x.astype(F32)
    scale = lax.rsqrt(jnp.mean(wide * wide, axis=-1, keepdims=True) + EPS)
    return ((wide * scale * gain).astype(BF16), scale)


def eye_mask(order):
    rows = lax.broadcasted_iota(jnp.int32, (order, order), 0)
    return rows == lax.broadcasted_iota(jnp.int32, (order, order), 1)


def step_coefficients(low, high):
    mid, half = (low + high) * 0.5, (high - low) * 0.5
    scale = 1.0 / (2.0 * mid * mid - half * half)
    return 4.0 * mid * scale, 2.0 * scale, half * half * scale


def split(value):
    high = value.astype(BF16)
    rest = value - high.astype(F32)
    middle = rest.astype(BF16)
    return high, middle, (rest - middle.astype(F32)).astype(BF16)


def dot_three(a, b):
    a_high, a_low, _ = split(a)
    b_high, b_low, _ = split(b)
    low = dot(a_low, b_high, precision=None) + dot(a_high, b_low, precision=None)
    return low + dot(a_high, b_high, precision=None)


def largest_of(values):
    largest = values[0]
    for value in values[1:]:
        largest = jnp.maximum(largest, value)
    return largest


def fourth_root(square):
    return jnp.sqrt(jnp.sqrt(jnp.sum(square * square)))


def invert(matrices, low, state, product, polish):
    order = matrices[0].shape[0]
    eye = eye_mask(order).astype(F32)
    spreads = []
    for index, matrix in enumerate(matrices):
        square = product(matrix, matrix)
        high = jnp.maximum(fourth_root(square), low) * 1.001
        first, second, spread = step_coefficients(low, high)
        state[index, :order] = first * eye - second * matrix
        state[index, order:] = first * matrix - second * square
        spreads.append(spread)

    def step(spreads):
        later = []
        for index, spread in enumerate(spreads):
            first, second, after = step_coefficients(1.0 - spread, 1.0 + spread)
            both = state[index]
            state[index] = first * both - second * product(both, both[order:])
            later.append(after)
        return tuple(later)

    lax.while_loop(lambda spreads: largest_of(spreads) > 2e-3, step, tuple(spreads))
    guesses = [state[index, :order] for index in range(len(matrices))]
    for _ in range(polish):
        residuals = [eye - dot(m, g) for g, m in zip(guesses, matrices)]
        guesses = [g + product(g, r) for g, r in zip(guesses, residuals)]
    return guesses


def invert_by_halves(factor, count, damping, state):
    half = factor.shape[1] // 2
    every = range(count)
    corner = [factor[i, :half, :half] for i in every]
    upper = [factor[i, :half, half:] for i in every]
    inverse = invert(corner, damping, state, dot_three, 1)
    tall = [dot(inverse[i], upper[i]) for i in every]
    error = [dot(corner[i], tall[i]) - upper[i] for i in every]
    tall = [tall[i] - dot_three(inverse[i], error[i]) for i in every]
    error = [dot(corner[i], tall[i]) - upper[i] for i in every]
    rest = [
        factor[i, half:, half:] - dot(tall[i].T, upper[i] - error[i]) for i in every
    ]
    rest = invert(rest, damping, state, dot_three, 1)
    for i in every:
        cross = dot(tall[i], rest[i])
        factor[i, :half, :half] = inverse[i] + dot(cross, tall[i], (1, 1))
        factor[i, :half, half:] = -cross
        factor[i, half:, :half] = -cross.T
        factor[i, half:, half:] = rest[i]


def apply_inverse(blocks, damping, factor, state, whole, load, store):
    rows_list = [load(i, 0, BLOCK) for i in range(blocks)]
    count = rows_list[0].shape[0]
    half = count // 2
    eye = eye_mask(count)
    squares = []
    for index, rows in enumerate(rows_list):
        gram = dot(rows, rows, (1, 1), None) * (1.0 / count)
        factor[index] = jnp.where(eye, gram + damping, gram)
        for corner in (gram[:half, :half].astype(BF16), gram[half:, half:].astype(BF16)):
            squares.append(dot(corner, corner, precision=None))
    easy = fourth_root(largest_of([jnp.abs(square) for square in squares])) < HARDEST * damping

    @pl.when(easy)
    def _():
        invert_by_halves(factor, len(rows_list), damping, state)
        for i, rows in enumerate(rows_list):
            high, low, _ = split(factor[i])
            solved = dot(low, rows, precision=None)
            store(i, (solved + dot(high, rows, precision=None)).astype(BF16))

    @pl.when(jnp.logical_not(easy))
    def _():
        def one(i, carry):
            matrix = factor[pl.ds(i, 1)][0]
            (inverse,) = invert([matrix], damping, whole, dot, 3)
            for start in range(0, BLOCK, 256):
                exact = load(i, start, 256).astype(F32)
                solved = dot(inverse, exact)
                solved = solved + dot(inverse, exact - dot(matrix, solved))
                store(i, solved.astype(BF16), start)
            return carry

        lax.fori_loop(0, len(rows_list), one, 0)


HARDEST = 2e4


OWNERS = (0, 2, 4, 5, 7)
UNIT = 128
MOVES = (
    (5, {0: 0, 2: 2, 4: 3, 5: 1, 7: 3}, {0: 0, 2: 0, 4: -1, 5: 0, 7: 0}),
    (4, {0: 4, 4: 0, 7: 0}, {1: -1, 3: 1, 6: 2}),
    (2, {2: 0, 5: 6}, {1: 3, 6: 0}),
    (1, {2: 7, 5: 0}, {3: 0, 4: 4}),
)
PAIRS = (None, ((0, 1), (4, 3), (7, 6)), ((2, 1), (5, 6)), ((2, 3), (5, 4)))
WINDOW = 5


def lookup(table, missing, me):
    value = jnp.int32(missing)
    for device, entry in table.items():
        value = jnp.where(me == device, entry, value)
    return value


def act_kernel(damping_ref, me_ref, rows_ref, left_ref, *refs):
    moves, (solved_ref, factor, state, whole) = refs[: len(MOVES)], refs[len(MOVES) :]

    def load(_, start, size):
        return rows_ref[:, start : start + size]

    def store(_, solved, start=0):
        solved_ref[:, start : start + solved.shape[1]] = solved

    apply_inverse(1, damping_ref[0, 0], factor, state, whole, load, store)
    left_ref[...] = dot(solved_ref[...], rows_ref[:, :BLOCK], (1, 1), None)
    for (units, first, _), out in zip(MOVES, moves):
        start = pl.multiple_of(lookup(first, 0, me_ref[0, 0]) * UNIT, UNIT)
        out[...] = solved_ref[:, pl.ds(start, units * UNIT)]


def assemble_kernel(me_ref, *refs):
    moves, (out_ref, buffer) = refs[: len(MOVES)], refs[len(MOVES) :]
    for (units, _, place), piece in zip(MOVES, moves):
        start = (lookup(place, WINDOW + 1, me_ref[0, 0]) + 1) * UNIT
        buffer[:, pl.ds(pl.multiple_of(start, UNIT), units * UNIT)] = piece[...]
    out_ref[...] = buffer[:, UNIT : (WINDOW + 1) * UNIT].T


def grad_kernel(damping_ref, rows_ref, left_ref, solved_ref, term_ref, factor, state, whole):
    blocks = rows_ref.shape[1] // BLOCK

    def columns(index, start, size):
        if isinstance(index, int):
            return slice(index * BLOCK + start, index * BLOCK + start + size)
        return pl.ds(pl.multiple_of(index * BLOCK + start, 128), size)

    def load(index, start, size):
        return rows_ref[:, columns(index, start, size)]

    def store(index, solved, start=0):
        solved_ref[:, columns(index, start, solved.shape[1])] = solved

    apply_inverse(blocks, damping_ref[0, 0], factor, state, whole, load, store)
    right = dot(solved_ref[...], rows_ref[...], (1, 1), None)
    product = jnp.sum(left_ref[...] * right, axis=0, keepdims=True)
    term_ref[...] = jnp.sum(product, axis=1, keepdims=True)


VMEM = pl.BlockSpec(memory_space=pltpu.VMEM)
SMEM = pl.BlockSpec(memory_space=pltpu.SMEM)


def solve_act(damping, me, rows):
    count = rows.shape[0]
    return pl.pallas_call(
        act_kernel,
        out_shape=(jax.ShapeDtypeStruct((count, count), F32),)
        + tuple(jax.ShapeDtypeStruct((count, units * UNIT), BF16) for units, _, _ in MOVES),
        in_specs=[SMEM, SMEM, VMEM],
        out_specs=(VMEM,) * (len(MOVES) + 1),
        scratch_shapes=[
            pltpu.VMEM((count, BLOCK), BF16),
            pltpu.VMEM((1, count, count), F32),
            pltpu.VMEM((1, count, count // 2), F32),
            pltpu.VMEM((1, 2 * count, count), F32),
        ],
        compiler_params=pltpu.CompilerParams(vmem_limit_bytes=28 * 2**20),
        cost_estimate=pl.CostEstimate(
            flops=16 * 10**9, bytes_accessed=4 * 2**20, transcendentals=0
        ),
        name="solve_act",
    )(damping, me, rows)


def solve_grad(damping, rows, left):
    count, width = rows.shape
    blocks = width // BLOCK
    return pl.pallas_call(
        grad_kernel,
        out_shape=(
            jax.ShapeDtypeStruct((count, width), BF16),
            jax.ShapeDtypeStruct((1, 1), F32),
        ),
        in_specs=[SMEM, VMEM, VMEM],
        out_specs=(VMEM, VMEM),
        scratch_shapes=[
            pltpu.VMEM((blocks, count, count), F32),
            pltpu.VMEM((blocks, count, count // 2), F32),
            pltpu.VMEM((1, 2 * count, count), F32),
        ],
        compiler_params=pltpu.CompilerParams(vmem_limit_bytes=40 * 2**20),
        cost_estimate=pl.CostEstimate(
            flops=45 * 10**9, bytes_accessed=8 * 2**20, transcendentals=0
        ),
        name="solve_grad",
    )(damping, rows, left)


def swap(value, offset):
    return lax.ppermute(value, "dp", [(i, i ^ offset) for i in range(8)])


def gather_pieces(value):
    half = value.shape[0] // 2
    other = swap(value, 4)
    direct = [swap(value, 1), swap(value, 3), swap(other, 1), swap(other, 3)]
    pieces, places = [value, other] + direct, [(0, 0), (4, 0), (1, 0), (3, 0), (5, 0), (7, 0)]
    for near, far, offset in ((direct[0], direct[1], 2), (direct[2], direct[3], 6)):
        pieces += [swap(far[:half], 1), swap(near[half:], 3)]
        places += [(offset, 0), (offset, half)]
    return pieces, places


def normalize_kernel(fwd_ref, bwd_ref, gain_ref, out_ref):
    gain = gain_ref[...]
    normed_b, _ = normalize(bwd_ref[...], gain)
    normed_f, _ = normalize(fwd_ref[...], gain)
    part = normed_f.shape[1] // out_ref.shape[0]
    for device in range(out_ref.shape[0]):
        if device in OWNERS:
            block = OWNERS.index(device)
            out_ref[device, :, :BLOCK] = normed_b[:, block * BLOCK : (block + 1) * BLOCK]
        else:
            out_ref[device, :, :BLOCK] = jnp.zeros((normed_b.shape[0], BLOCK), BF16)
        out_ref[device, :, BLOCK:] = normed_f[:, device * part : (device + 1) * part]


def product_kernel(places, me_ref, *refs):
    me = me_ref[0, 0]
    pieces, (rows_ref, weight_ref, gathered, out_ref) = refs[: len(places)], refs[len(places) :]
    groups, tokens, _ = out_ref.shape
    width = weight_ref.shape[1]
    for piece, (offset, first) in zip(pieces, places):
        start = pl.multiple_of((me ^ offset) * tokens + first, 32)
        gathered[pl.ds(start, piece.shape[0]), :] = piece[...]
    weight = weight_ref[...]
    for pair in range(0, groups, 2):
        rows = slice(pair * tokens, (pair + 2) * tokens)
        forward = dot(rows_ref[rows, BLOCK:], weight, precision=None).astype(BF16)
        backward = dot(gathered[rows, :], weight, (1, 1), None).astype(BF16)
        for device in range(2):
            own = slice(device * tokens, (device + 1) * tokens)
            out_ref[pair + device, :, :width] = forward[own]
            out_ref[pair + device, :, width:] = backward[own]


def finish_kernel(parts_ref, fwd_ref, bwd_ref, grad_ref, gain_ref, next_ref, back_ref):
    groups = parts_ref.shape[0]
    width = fwd_ref.shape[1]
    part = width // groups
    out_width = parts_ref.shape[2] - part
    layer = parts_ref[0, :, :out_width].astype(F32)
    for group in range(1, groups):
        layer += parts_ref[group, :, :out_width].astype(F32)
    next_ref[:, :out_width] = (fwd_ref[:, :out_width].astype(F32) + layer).astype(BF16)
    next_ref[:, out_width:] = fwd_ref[:, out_width:]
    wide = bwd_ref[...].astype(F32)
    scale = lax.rsqrt(jnp.mean(wide * wide, axis=-1, keepdims=True) + EPS)
    back = jnp.concatenate([parts_ref[group, :, out_width:] for group in range(groups)], axis=1)
    scaled = back.astype(F32) * gain_ref[...]
    inner = jnp.mean(scaled * wide, axis=-1, keepdims=True)
    out = grad_ref[...].astype(F32) + scale * scaled - wide * scale**3 * inner
    back_ref[...] = out.astype(BF16)


def update_kernel(entries, terms_ref, turned_ref, grad_ref, out_ref):
    terms = terms_ref[...]
    total = jnp.sum(jnp.sum(terms, axis=0, keepdims=True)[:, :1], axis=1, keepdims=True)
    ratio = jnp.sqrt(entries / total)
    out_ref[...] = (ratio * dot(turned_ref[...], grad_ref[...], precision=None)).astype(BF16)


def shape(*dims, dtype=BF16):
    return jax.ShapeDtypeStruct(dims, dtype)


def cost(flops, moved):
    return pl.CostEstimate(flops=flops, bytes_accessed=moved, transcendentals=0)


def params(mib):
    return pltpu.CompilerParams(vmem_limit_bytes=mib * 2**20)


def per_device(x_fwd, x_bwd, grad_in, gain, weight, damping):
    fwd = x_fwd[0]
    bwd = x_bwd[0]
    grad = grad_in[0]
    local_w = weight[0]
    tokens, width = fwd.shape
    own_rows, out_width = local_w.shape
    groups = lax.axis_size("dp")
    group = groups * tokens
    me = lax.axis_index("dp")
    me_value = me.reshape(1, 1)
    damp_value = damping.reshape(1, 1)

    pieces, places = gather_pieces(grad[:, :out_width])

    sent = pl.pallas_call(
        normalize_kernel,
        out_shape=shape(groups, tokens, BLOCK + own_rows),
        in_specs=[VMEM] * 3,
        out_specs=VMEM,
        compiler_params=params(32),
        cost_estimate=cost(10**7, 3 * 10**6),
        name="normalize",
    )(fwd, bwd, gain)
    rows = lax.all_to_all(sent, "dp", 0, 0, tiled=True).reshape(group, BLOCK + own_rows)

    rows_late, *_ = lax.optimization_barrier((rows, pieces[1], *pieces[6:8]))
    left, *moves = solve_act(damp_value, me_value, rows_late)

    ready = lax.optimization_barrier((me_value, *pieces, rows, left))
    group_grad, products = pl.pallas_call(
        lambda *refs: product_kernel(places, *refs),
        out_shape=(shape(group, out_width), shape(groups, tokens, out_width + own_rows)),
        in_specs=[SMEM] + [VMEM] * (len(pieces) + 2),
        out_specs=(VMEM,) * 2,
        compiler_params=params(40),
        cost_estimate=cost(4 * 10**9, 10**7),
        name="products",
    )(*ready[:-1], local_w)
    parts = lax.all_to_all(products, "dp", 0, 0, tiled=True)

    moves = moves[:1] + [
        lax.ppermute(piece, "dp", pairs) for piece, pairs in zip(moves[1:], PAIRS[1:])
    ]
    turned = pl.pallas_call(
        assemble_kernel,
        out_shape=shape(own_rows, group),
        in_specs=[SMEM] + [VMEM] * len(MOVES),
        out_specs=VMEM,
        scratch_shapes=[pltpu.VMEM((group, (2 * WINDOW + 2) * UNIT), BF16)],
        compiler_params=params(16),
        cost_estimate=cost(10**7, 3 * 10**6),
        name="assemble",
    )(me_value, *moves)

    grad_tilde, term = solve_grad(damp_value, group_grad, left)
    devices = lax.axis_size("section") * groups
    terms = lax.all_to_all(
        jnp.broadcast_to(term, (devices, 128)), ("section", "dp"), 0, 0, tiled=True
    )

    parts, _ = lax.optimization_barrier((parts, term))
    out_f, out_b = pl.pallas_call(
        finish_kernel,
        out_shape=(shape(tokens, width),) * 2,
        in_specs=[VMEM] * 5,
        out_specs=(VMEM,) * 2,
        compiler_params=params(32),
        cost_estimate=cost(10**7, 8 * 10**6),
        name="finish",
    )(parts, fwd, bwd, grad, gain)
    next_fwd = from_behind(out_f, "section", 1)
    next_grad = from_behind(out_b, "section", -1)

    columns = 512
    entries = float(lax.axis_size("section") * width * out_width)
    update = pl.pallas_call(
        lambda *refs: update_kernel(entries, *refs),
        grid=(out_width // columns,),
        out_shape=shape(own_rows, out_width),
        in_specs=[
            pl.BlockSpec((devices, 128), lambda i: (0, 0)),
            pl.BlockSpec((own_rows, group), lambda i: (0, 0)),
            pl.BlockSpec((group, columns), lambda i: (0, i)),
        ],
        out_specs=pl.BlockSpec((own_rows, columns), lambda i: (0, i)),
        compiler_params=params(32),
        cost_estimate=cost(2 * 10**9, 8 * 10**6),
        name="update",
    )(terms, turned, grad_tilde)
    return (next_fwd[None], next_grad[None], update[None])


def solution(mesh):
    return jax.shard_map(
        per_device,
        mesh=mesh,
        in_specs=(
            P("section", "dp", None),
            P("section", "dp", None),
            P("section", "dp", None),
            P("section", None),
            P("section", "dp", None),
            P("section"),
        ),
        out_specs=(P("section", "dp", None), P("section", "dp", None), P("section", "dp", None)),
        check_vma=False,
    )
```

```python
import jax
import jax.numpy as jnp
from jax import lax
from jax.experimental import pallas as pl
from jax.experimental.pallas import tpu as pltpu
from jax.sharding import PartitionSpec as P

BLOCK = 1024
EPS = 1e-06
F32 = jnp.float32
BF16 = jnp.bfloat16
EXACT = lax.Precision.HIGHEST


def dot(a, b, contract=(1, 0), precision=EXACT):
    return lax.dot_general(
        a,
        b,
        (((contract[0],), (contract[1],)), ((), ())),
        precision=precision,
        preferred_element_type=F32,
    )


def from_behind(value, axis, steps):
    count = lax.axis_size(axis)
    leading, last = (max(0, -steps), min(count, count - steps))
    return lax.ppermute(value, axis, [(source, source + steps) for source in range(leading, last)])


def normalize(x, gain):
    wide = x.astype(F32)
    scale = lax.rsqrt(jnp.mean(wide * wide, axis=-1, keepdims=True) + EPS)
    return ((wide * scale * gain).astype(BF16), scale)


def eye_mask(order):
    rows = lax.broadcasted_iota(jnp.int32, (order, order), 0)
    return rows == lax.broadcasted_iota(jnp.int32, (order, order), 1)


def step_coefficients(low, high):
    mid, half = (low + high) * 0.5, (high - low) * 0.5
    scale = 1.0 / (2.0 * mid * mid - half * half)
    return 4.0 * mid * scale, 2.0 * scale, half * half * scale


def split(value):
    high = value.astype(BF16)
    rest = value - high.astype(F32)
    middle = rest.astype(BF16)
    return high, middle, (rest - middle.astype(F32)).astype(BF16)


def dot_three(a, b):
    a_high, a_low, _ = split(a)
    b_high, b_low, _ = split(b)
    low = dot(a_low, b_high, precision=None) + dot(a_high, b_low, precision=None)
    return low + dot(a_high, b_high, precision=None)


def fourth_root(square):
    return jnp.sqrt(jnp.sqrt(jnp.sum(square * square)))


def by_rows(count, step, body):
    def one(index, carry):
        body(pl.ds(pl.multiple_of(index * step, step), step))
        return carry

    lax.fori_loop(0, count // step, one, 0)


def scaled_newton(spread, step):
    def once(spread):
        first, second, after = step_coefficients(1.0 - spread, 1.0 + spread)
        step(first, second)
        return after

    lax.while_loop(lambda spread: spread > 2e-2, once, spread)


def invert(matrix, low, state):
    order = matrix.shape[0]
    eye = eye_mask(order).astype(F32)
    square = dot(matrix, matrix)
    high = jnp.maximum(fourth_root(square), low) * 1.001
    first, second, spread = step_coefficients(low, high)
    state[:order] = first * eye - second * matrix
    state[order:] = first * matrix - second * square

    def step(first, second):
        both = state[...]
        state[...] = first * both - second * dot_three(both, both[order:])

    scaled_newton(spread, step)
    guess = state[:order]
    return guess + dot_three(guess, eye - dot(matrix, guess))


def invert_by_halves(factor, damping, state, parts):
    half = factor.shape[0] // 2
    parts[0] = factor[:half, :half]

    def stage(index, carry):
        inverse = invert(parts[index], damping, state)

        @pl.when(index == 0)
        def _():
            corner, upper = parts[0], factor[:half, half:]
            tall = dot(inverse, upper)

            parts[3] = tall - dot(inverse, dot(corner, tall) - upper)
            tall = parts[3]
            error = dot(corner, tall) - upper
            parts[1] = factor[half:, half:] - dot(tall.T, upper - error)

            parts[2] = inverse

        @pl.when(index == 1)
        def _():
            parts[1] = inverse

        return carry

    lax.fori_loop(0, 2, stage, 0)
    inverse, tall, rest = parts[2], parts[3], parts[1]
    cross = dot(tall, rest)
    factor[:half, :half] = inverse + dot(cross, tall.T)
    factor[:half, half:] = -cross
    factor[half:, :half] = -cross.T
    factor[half:, half:] = rest


def invert_whole(factor, damping, whole, spare):
    order = factor.shape[0]
    eye = eye_mask(order).astype(F32)

    def square(rows):
        spare[rows] = dot(factor[rows], factor[...])

    by_rows(order, 128, square)
    high = jnp.maximum(fourth_root(spare[...]), damping) * 1.001
    first, second, spread = step_coefficients(damping, high)
    whole[:order] = first * eye - second * factor[...]
    whole[order:] = first * factor[...] - second * spare[...]

    def step(first, second):
        spare[...] = whole[order:]

        def some(rows):
            whole[rows] = first * whole[rows] - second * dot(whole[rows], spare[...])

        by_rows(2 * order, 128, some)

    scaled_newton(spread, step)

    def polish(_, carry):
        def residual(rows):
            spare[rows] = dot(factor[rows], whole[:order])

        by_rows(order, 128, residual)
        spare[...] = eye - spare[...]

        def correct(rows):
            whole[rows] += dot(whole[rows], spare[...])

        by_rows(order, 128, correct)
        return carry

    lax.fori_loop(0, 3, polish, 0)


def apply_inverse(damping, rows_ref, columns, out_ref, out_columns, scratch):
    factor, state, parts, whole, spare = scratch
    count = rows_ref.shape[0]
    half = count // 2
    width = 256

    def gram(rows):
        factor[rows] = dot(rows_ref[rows, columns(0, BLOCK)], rows_ref[:, columns(0, BLOCK)], (1, 1), None) * (
            1.0 / count
        )

    by_rows(count, half, gram)
    squares = []
    for corner in (factor[:half, :half], factor[half:, half:]):
        corner = corner.astype(BF16)
        squares.append(jnp.abs(dot(corner, corner, precision=None)))
    easy = fourth_root(jnp.maximum(*squares)) < HARDEST * damping
    factor[...] = jnp.where(eye_mask(count), factor[...] + damping, factor[...])

    @pl.when(easy)
    def _():
        invert_by_halves(factor, damping, state, parts)

        def solve(rows):
            high, low, _ = split(factor[rows])
            block = rows_ref[:, columns(0, BLOCK)]
            solved = dot(low, block, precision=None) + dot(high, block, precision=None)
            out_ref[rows, out_columns(0, BLOCK)] = solved.astype(BF16)

        by_rows(count, half, solve)

    @pl.when(jnp.logical_not(easy))
    def _():
        invert_whole(factor, damping, whole, spare)

        def solve(index, carry):
            start = index * width
            exact = rows_ref[:, columns(start, width)].astype(F32)

            def guess(rows):
                spare[rows, :width] = dot(whole[rows], exact)

            def residual(rows):
                spare[rows, width:] = dot(factor[rows], spare[:, :width])

            def correct(rows):
                fixed = spare[rows, :width] + dot(whole[rows], spare[:, width:])
                out_ref[rows, out_columns(start, width)] = fixed.astype(BF16)

            by_rows(count, 128, guess)
            by_rows(count, 128, residual)
            spare[:, width:] = exact - spare[:, width:]
            by_rows(count, 128, correct)
            return carry

        lax.fori_loop(0, BLOCK // width, solve, 0)


HARDEST = 2e4
ACT_MIB = 18
GRAD_MIB = 24


def solver_scratch(count):
    half = count // 2
    return [
        pltpu.VMEM((count, count), F32),
        pltpu.VMEM((count, half), F32),
        pltpu.VMEM((4, half, half), F32),
        pltpu.VMEM((2 * count, count), F32),
        pltpu.VMEM((count, count), F32),
    ]


OWNERS = (0, 2, 4, 5, 7)
UNIT = 128
MOVES = (
    (5, {0: 0, 2: 2, 4: 3, 5: 1, 7: 3}, {0: 0, 2: 0, 4: -1, 5: 0, 7: 0}),
    (4, {0: 4, 4: 0, 7: 0}, {1: -1, 3: 1, 6: 2}),
    (2, {2: 0, 5: 6}, {1: 3, 6: 0}),
    (1, {2: 7, 5: 0}, {3: 0, 4: 4}),
)
PAIRS = (None, ((0, 1), (4, 3), (7, 6)), ((2, 1), (5, 6)), ((2, 3), (5, 4)))
WINDOW = 5


def lookup(table, missing, me):
    value = jnp.int32(missing)
    for device, entry in table.items():
        value = jnp.where(me == device, entry, value)
    return value


def act_kernel(damping_ref, me_ref, rows_ref, left_ref, *refs):
    moves, (solved_ref, *scratch) = refs[: len(MOVES)], refs[len(MOVES) :]

    def columns(start, size):
        return slice(start, start + size) if isinstance(start, int) else pl.ds(start, size)

    apply_inverse(damping_ref[0, 0], rows_ref, columns, solved_ref, columns, scratch)

    def compare(rows):
        left_ref[rows] = dot(solved_ref[rows, :], rows_ref[:, :BLOCK], (1, 1), None)

    by_rows(solved_ref.shape[0], 256, compare)
    for (units, first, _), out in zip(MOVES, moves):
        start = pl.multiple_of(lookup(first, 0, me_ref[0, 0]) * UNIT, UNIT)
        out[...] = solved_ref[:, pl.ds(start, units * UNIT)]


def assemble_kernel(me_ref, *refs):
    moves, (out_ref, buffer) = refs[: len(MOVES)], refs[len(MOVES) :]
    for (units, _, place), piece in zip(MOVES, moves):
        start = (lookup(place, WINDOW + 1, me_ref[0, 0]) + 1) * UNIT
        buffer[:, pl.ds(pl.multiple_of(start, UNIT), units * UNIT)] = piece[...]
    out_ref[...] = buffer[:, UNIT : (WINDOW + 1) * UNIT].T


def grad_kernel(damping_ref, rows_ref, left_ref, solved_ref, term_ref, right, *scratch):
    count, width = rows_ref.shape

    def one(index, carry):
        def columns(start, size):
            return pl.ds(pl.multiple_of(index * BLOCK + start, UNIT), size)

        apply_inverse(damping_ref[0, 0], rows_ref, columns, solved_ref, columns, scratch)
        return carry

    lax.fori_loop(0, width // BLOCK, one, 0)

    def compare(rows):
        product = dot(solved_ref[rows, :], rows_ref[...], (1, 1), None)
        right[rows] = product * left_ref[rows]

    by_rows(count, 256, compare)
    product = jnp.sum(right[...], axis=0, keepdims=True)
    term_ref[...] = jnp.sum(product, axis=1, keepdims=True)


VMEM = pl.BlockSpec(memory_space=pltpu.VMEM)
SMEM = pl.BlockSpec(memory_space=pltpu.SMEM)


def solve_act(damping, me, rows):
    count = rows.shape[0]
    return pl.pallas_call(
        act_kernel,
        out_shape=(jax.ShapeDtypeStruct((count, count), F32),)
        + tuple(jax.ShapeDtypeStruct((count, units * UNIT), BF16) for units, _, _ in MOVES),
        in_specs=[SMEM, SMEM, VMEM],
        out_specs=(VMEM,) * (len(MOVES) + 1),
        scratch_shapes=[pltpu.VMEM((count, BLOCK), BF16)] + solver_scratch(count),
        compiler_params=pltpu.CompilerParams(vmem_limit_bytes=ACT_MIB * 2**20),
        cost_estimate=pl.CostEstimate(
            flops=16 * 10**9, bytes_accessed=4 * 2**20, transcendentals=0
        ),
        name="solve_act",
    )(damping, me, rows)


def solve_grad(damping, rows, left):
    count, width = rows.shape
    return pl.pallas_call(
        grad_kernel,
        out_shape=(
            jax.ShapeDtypeStruct((count, width), BF16),
            jax.ShapeDtypeStruct((1, 1), F32),
        ),
        in_specs=[SMEM, VMEM, VMEM],
        out_specs=(VMEM, VMEM),
        scratch_shapes=[pltpu.VMEM((count, count), F32)] + solver_scratch(count),
        compiler_params=pltpu.CompilerParams(vmem_limit_bytes=GRAD_MIB * 2**20),
        cost_estimate=pl.CostEstimate(
            flops=45 * 10**9, bytes_accessed=8 * 2**20, transcendentals=0
        ),
        name="solve_grad",
    )(damping, rows, left)


def swap(value, offset):
    return lax.ppermute(value, "dp", [(i, i ^ offset) for i in range(8)])


def normalize_kernel(fwd_ref, bwd_ref, gain_ref, out_ref):
    gain = gain_ref[...]
    normed_b, _ = normalize(bwd_ref[...], gain)
    normed_f, _ = normalize(fwd_ref[...], gain)
    part = normed_f.shape[1] // out_ref.shape[0]
    for device in range(out_ref.shape[0]):
        if device in OWNERS:
            block = OWNERS.index(device)
            out_ref[device, :, :BLOCK] = normed_b[:, block * BLOCK : (block + 1) * BLOCK]
        else:
            out_ref[device, :, :BLOCK] = jnp.zeros((normed_b.shape[0], BLOCK), BF16)
        out_ref[device, :, BLOCK:] = normed_f[:, device * part : (device + 1) * part]


def product_kernel(me_ref, *refs):
    me = me_ref[0, 0]
    pieces, (rows_ref, weight_ref, gathered, out_ref) = refs[:-4], refs[-4:]
    groups, tokens, _ = out_ref.shape
    part, width = weight_ref.shape
    for offset, piece in enumerate(pieces):
        start = pl.multiple_of((me ^ offset) * tokens, tokens)
        gathered[pl.ds(start, tokens), :] = piece[...]
    for start in range(0, width, 512):
        columns = slice(start, start + 512)
        forward = dot(rows_ref[:, BLOCK:], weight_ref[:, columns], precision=None)
        out_ref[:, :, columns] = forward.astype(BF16).reshape(groups, tokens, 512)
    backward = dot(gathered[...], weight_ref[...], (1, 1), None)
    out_ref[:, :, width:] = backward.astype(BF16).reshape(groups, tokens, part)


def finish_kernel(parts_ref, fwd_ref, bwd_ref, grad_ref, gain_ref, next_ref, back_ref):
    groups = parts_ref.shape[0]
    width = fwd_ref.shape[1]
    part = width // groups
    out_width = parts_ref.shape[2] - part
    layer = parts_ref[0, :, :out_width].astype(F32)
    for group in range(1, groups):
        layer += parts_ref[group, :, :out_width].astype(F32)
    next_ref[0, :, :out_width] = (fwd_ref[:, :out_width].astype(F32) + layer).astype(BF16)
    next_ref[0, :, out_width:] = fwd_ref[:, out_width:]
    wide = bwd_ref[...].astype(F32)
    scale = lax.rsqrt(jnp.mean(wide * wide, axis=-1, keepdims=True) + EPS)
    back = jnp.concatenate([parts_ref[group, :, out_width:] for group in range(groups)], axis=1)
    scaled = back.astype(F32) * gain_ref[...]
    inner = jnp.mean(scaled * wide, axis=-1, keepdims=True)
    out = grad_ref[...].astype(F32) + scale * scaled - wide * scale**3 * inner
    back_ref[0] = out.astype(BF16)


def update_kernel(entries, terms_ref, turned_ref, grad_ref, out_ref):
    terms = terms_ref[...]
    total = jnp.sum(jnp.sum(terms, axis=0, keepdims=True)[:, :1], axis=1, keepdims=True)
    ratio = jnp.sqrt(entries / total)
    out_ref[...] = (ratio * dot(turned_ref[...], grad_ref[...], precision=None)).astype(BF16)


def shape(*dims, dtype=BF16):
    return jax.ShapeDtypeStruct(dims, dtype)


def cost(flops, moved):
    return pl.CostEstimate(flops=flops, bytes_accessed=moved, transcendentals=0)


def params(mib):
    return pltpu.CompilerParams(vmem_limit_bytes=mib * 2**20)


def per_device(x_fwd, x_bwd, grad_in, gain, weight, damping):
    fwd = x_fwd[0]
    bwd = x_bwd[0]
    grad = grad_in[0]
    local_w = weight[0]
    tokens, width = fwd.shape
    own_rows, out_width = local_w.shape
    groups = lax.axis_size("dp")
    group = groups * tokens
    me = lax.axis_index("dp")
    me_value = me.reshape(1, 1)
    damp_value = damping.reshape(1, 1)

    upstream = grad[:, :out_width]
    pieces = [upstream] + [swap(upstream, offset) for offset in range(1, groups)]

    sent = pl.pallas_call(
        normalize_kernel,
        out_shape=shape(groups, tokens, BLOCK + own_rows),
        in_specs=[VMEM] * 3,
        out_specs=VMEM,
        compiler_params=params(32),
        cost_estimate=cost(10**7, 3 * 10**6),
        name="normalize",
    )(fwd, bwd, gain)
    rows = lax.all_to_all(sent, "dp", 0, 0, tiled=True).reshape(group, BLOCK + own_rows)

    left, *moves = solve_act(damp_value, me_value, rows)

    ready = lax.optimization_barrier((me_value, *pieces, rows, left))
    group_grad, products = pl.pallas_call(
        product_kernel,
        out_shape=(shape(group, out_width), shape(groups, tokens, out_width + own_rows)),
        in_specs=[SMEM] + [VMEM] * (len(pieces) + 2),
        out_specs=(VMEM,) * 2,
        compiler_params=params(40),
        cost_estimate=cost(4 * 10**9, 10**7),
        name="products",
    )(*ready[:-1], local_w)
    parts = lax.all_to_all(products, "dp", 0, 0, tiled=True)

    moves = moves[:1] + [
        lax.ppermute(piece, "dp", pairs) for piece, pairs in zip(moves[1:], PAIRS[1:])
    ]
    turned = pl.pallas_call(
        assemble_kernel,
        out_shape=shape(own_rows, group),
        in_specs=[SMEM] + [VMEM] * len(MOVES),
        out_specs=VMEM,
        scratch_shapes=[pltpu.VMEM((group, (2 * WINDOW + 2) * UNIT), BF16)],
        compiler_params=params(16),
        cost_estimate=cost(10**7, 3 * 10**6),
        name="assemble",
    )(me_value, *moves)

    grad_tilde, term = solve_grad(damp_value, group_grad, left)
    devices = lax.axis_size("section") * groups
    terms = lax.all_to_all(
        jnp.broadcast_to(term, (devices, 128)), ("section", "dp"), 0, 0, tiled=True
    )

    parts, _ = lax.optimization_barrier((parts, term))
    out_f, out_b = pl.pallas_call(
        finish_kernel,
        out_shape=(shape(1, tokens, width),) * 2,
        in_specs=[VMEM] * 5,
        out_specs=(VMEM,) * 2,
        compiler_params=params(32),
        cost_estimate=cost(10**7, 8 * 10**6),
        name="finish",
    )(parts, fwd, bwd, grad, gain)
    next_fwd = from_behind(out_f, "section", 1)
    next_grad = from_behind(out_b, "section", -1)

    columns = 512
    entries = float(lax.axis_size("section") * width * out_width)
    update = pl.pallas_call(
        lambda *refs: update_kernel(entries, *refs),
        grid=(out_width // columns,),
        out_shape=shape(own_rows, out_width),
        in_specs=[
            pl.BlockSpec((devices, 128), lambda i: (0, 0)),
            pl.BlockSpec((own_rows, group), lambda i: (0, 0)),
            pl.BlockSpec((group, columns), lambda i: (0, i)),
        ],
        out_specs=pl.BlockSpec((own_rows, columns), lambda i: (0, i)),
        compiler_params=params(32),
        cost_estimate=cost(2 * 10**9, 8 * 10**6),
        name="update",
    )(terms, turned, grad_tilde)
    return (next_fwd, next_grad, update[None])


def solution(mesh):
    return jax.shard_map(
        per_device,
        mesh=mesh,
        in_specs=(
            P("section", "dp", None),
            P("section", "dp", None),
            P("section", "dp", None),
            P("section", None),
            P("section", "dp", None),
            P("section"),
        ),
        out_specs=(P("section", "dp", None), P("section", "dp", None), P("section", "dp", None)),
        check_vma=False,
    )
```

```python
import jax
import jax.numpy as jnp
from jax import lax
from jax.experimental import pallas as pl
from jax.experimental.pallas import tpu as pltpu
from jax.sharding import PartitionSpec as P

BLOCK = 1024
EPS = 1e-06
F32 = jnp.float32
BF16 = jnp.bfloat16
EXACT = lax.Precision.HIGHEST


def dot(a, b, contract=(1, 0), precision=EXACT):
    return lax.dot_general(
        a,
        b,
        (((contract[0],), (contract[1],)), ((), ())),
        precision=precision,
        preferred_element_type=F32,
    )


def from_behind(value, axis, steps):
    count = lax.axis_size(axis)
    leading, last = (max(0, -steps), min(count, count - steps))
    return lax.ppermute(value, axis, [(source, source + steps) for source in range(leading, last)])


def normalize(x, gain):
    wide = x.astype(F32)
    scale = lax.rsqrt(jnp.mean(wide * wide, axis=-1, keepdims=True) + EPS)
    return ((wide * scale * gain).astype(BF16), scale)


def eye_mask(order):
    rows = lax.broadcasted_iota(jnp.int32, (order, order), 0)
    return rows == lax.broadcasted_iota(jnp.int32, (order, order), 1)


def step_coefficients(low, high):
    mid, half = (low + high) * 0.5, (high - low) * 0.5
    scale = 1.0 / (2.0 * mid * mid - half * half)
    return 4.0 * mid * scale, 2.0 * scale, half * half * scale


def split(value):
    high = value.astype(BF16)
    rest = value - high.astype(F32)
    middle = rest.astype(BF16)
    return high, middle, (rest - middle.astype(F32)).astype(BF16)


def dot_three(a, b):
    a_high, a_low, _ = split(a)
    b_high, b_low, _ = split(b)
    low = dot(a_low, b_high, precision=None) + dot(a_high, b_low, precision=None)
    return low + dot(a_high, b_high, precision=None)


def fourth_root(square):
    return jnp.sqrt(jnp.sqrt(jnp.sum(square * square)))


def by_rows(count, step, body):
    def one(index, carry):
        body(pl.ds(pl.multiple_of(index * step, step), step))
        return carry

    lax.fori_loop(0, count // step, one, 0)


def scaled_newton(spread, step):
    def once(spread):
        first, second, after = step_coefficients(1.0 - spread, 1.0 + spread)
        step(first, second)
        return after

    lax.while_loop(lambda spread: spread > 2e-2, once, spread)


def invert(matrix, low, state):
    order = matrix.shape[0]
    eye = eye_mask(order).astype(F32)
    square = dot(matrix, matrix)
    high = jnp.maximum(fourth_root(square), low) * 1.001
    first, second, spread = step_coefficients(low, high)
    state[:order] = first * eye - second * matrix
    state[order:] = first * matrix - second * square

    def step(first, second):
        both = state[...]
        state[...] = first * both - second * dot_three(both, both[order:])

    scaled_newton(spread, step)
    guess = state[:order]
    return guess + dot_three(guess, eye - dot(matrix, guess))


def invert_by_halves(factor, damping, state, parts):
    half = factor.shape[0] // 2
    parts[0] = factor[:half, :half]

    def stage(index, carry):
        inverse = invert(parts[index], damping, state)

        @pl.when(index == 0)
        def _():
            corner, upper = parts[0], factor[:half, half:]
            tall = dot(inverse, upper)

            parts[3] = tall - dot(inverse, dot(corner, tall) - upper)
            tall = parts[3]
            error = dot(corner, tall) - upper
            parts[1] = factor[half:, half:] - dot(tall.T, upper - error)

            parts[2] = inverse

        @pl.when(index == 1)
        def _():
            parts[1] = inverse

        return carry

    lax.fori_loop(0, 2, stage, 0)
    inverse, tall, rest = parts[2], parts[3], parts[1]
    cross = dot(tall, rest)
    factor[:half, :half] = inverse + dot(cross, tall.T)
    factor[:half, half:] = -cross
    factor[half:, :half] = -cross.T
    factor[half:, half:] = rest


def invert_whole(factor, damping, whole, spare):
    order = factor.shape[0]
    eye = eye_mask(order).astype(F32)

    def square(rows):
        spare[rows] = dot(factor[rows], factor[...])

    by_rows(order, 128, square)
    high = jnp.maximum(fourth_root(spare[...]), damping) * 1.001
    first, second, spread = step_coefficients(damping, high)
    whole[:order] = first * eye - second * factor[...]
    whole[order:] = first * factor[...] - second * spare[...]

    def step(first, second):
        spare[...] = whole[order:]

        def some(rows):
            whole[rows] = first * whole[rows] - second * dot(whole[rows], spare[...])

        by_rows(2 * order, 128, some)

    scaled_newton(spread, step)

    def polish(_, carry):
        def residual(rows):
            spare[rows] = dot(factor[rows], whole[:order])

        by_rows(order, 128, residual)
        spare[...] = eye - spare[...]

        def correct(rows):
            whole[rows] += dot(whole[rows], spare[...])

        by_rows(order, 128, correct)
        return carry

    lax.fori_loop(0, 3, polish, 0)


def apply_inverse(damping, rows_ref, columns, out_ref, out_columns, scratch):
    factor, state, parts, whole, spare = scratch
    count = rows_ref.shape[0]
    half = count // 2
    width = 256

    def gram(rows):
        factor[rows] = dot(rows_ref[rows, columns(0, BLOCK)], rows_ref[:, columns(0, BLOCK)], (1, 1), None) * (
            1.0 / count
        )

    by_rows(count, half, gram)
    squares = []
    for corner in (factor[:half, :half], factor[half:, half:]):
        corner = corner.astype(BF16)
        squares.append(jnp.abs(dot(corner, corner, precision=None)))
    easy = fourth_root(jnp.maximum(*squares)) < HARDEST * damping
    factor[...] = jnp.where(eye_mask(count), factor[...] + damping, factor[...])

    @pl.when(easy)
    def _():
        invert_by_halves(factor, damping, state, parts)

        def solve(rows):
            high, low, _ = split(factor[rows])
            block = rows_ref[:, columns(0, BLOCK)]
            solved = dot(low, block, precision=None) + dot(high, block, precision=None)
            out_ref[rows, out_columns(0, BLOCK)] = solved.astype(BF16)

        by_rows(count, half, solve)

    @pl.when(jnp.logical_not(easy))
    def _():
        invert_whole(factor, damping, whole, spare)

        def solve(index, carry):
            start = index * width
            exact = rows_ref[:, columns(start, width)].astype(F32)

            def guess(rows):
                spare[rows, :width] = dot(whole[rows], exact)

            def residual(rows):
                spare[rows, width:] = dot(factor[rows], spare[:, :width])

            def correct(rows):
                fixed = spare[rows, :width] + dot(whole[rows], spare[:, width:])
                out_ref[rows, out_columns(start, width)] = fixed.astype(BF16)

            by_rows(count, 128, guess)
            by_rows(count, 128, residual)
            spare[:, width:] = exact - spare[:, width:]
            by_rows(count, 128, correct)
            return carry

        lax.fori_loop(0, BLOCK // width, solve, 0)


HARDEST = 2e4
ACT_MIB = 14
GRAD_MIB = 16


def solver_scratch(count):
    half = count // 2
    return [
        pltpu.VMEM((count, count), F32),
        pltpu.VMEM((count, half), F32),
        pltpu.VMEM((4, half, half), F32),
        pltpu.VMEM((2 * count, count), F32),
        pltpu.VMEM((count, count), F32),
    ]


OWNERS = (0, 2, 4, 5, 7)
UNIT = 128
MOVES = (
    (5, {0: 0, 2: 2, 4: 3, 5: 1, 7: 3}, {0: 0, 2: 0, 4: -1, 5: 0, 7: 0}),
    (4, {0: 4, 4: 0, 7: 0}, {1: -1, 3: 1, 6: 2}),
    (2, {2: 0, 5: 6}, {1: 3, 6: 0}),
    (1, {2: 7, 5: 0}, {3: 0, 4: 4}),
)
PAIRS = (None, ((0, 1), (4, 3), (7, 6)), ((2, 1), (5, 6)), ((2, 3), (5, 4)))
WINDOW = 5


def lookup(table, missing, me):
    value = jnp.int32(missing)
    for device, entry in table.items():
        value = jnp.where(me == device, entry, value)
    return value


def act_kernel(damping_ref, me_ref, rows_ref, left_ref, *refs):
    moves, (solved_ref, *scratch) = refs[: len(MOVES)], refs[len(MOVES) :]

    def columns(start, size):
        return slice(start, start + size) if isinstance(start, int) else pl.ds(start, size)

    apply_inverse(damping_ref[0, 0], rows_ref, columns, solved_ref, columns, scratch)

    def compare(rows):
        left_ref[rows] = dot(solved_ref[rows, :], rows_ref[:, :BLOCK], (1, 1), None)

    by_rows(solved_ref.shape[0], 256, compare)
    for (units, first, _), out in zip(MOVES, moves):
        start = pl.multiple_of(lookup(first, 0, me_ref[0, 0]) * UNIT, UNIT)
        out[...] = solved_ref[:, pl.ds(start, units * UNIT)]


def assemble_kernel(me_ref, *refs):
    moves, (out_ref, buffer) = refs[: len(MOVES)], refs[len(MOVES) :]
    for (units, _, place), piece in zip(MOVES, moves):
        start = (lookup(place, WINDOW + 1, me_ref[0, 0]) + 1) * UNIT
        buffer[:, pl.ds(pl.multiple_of(start, UNIT), units * UNIT)] = piece[...]
    out_ref[...] = buffer[:, UNIT : (WINDOW + 1) * UNIT].T


def grad_kernel(damping_ref, rows_ref, left_ref, solved_ref, term_ref, right, *scratch):
    count, width = rows_ref.shape

    def one(index, carry):
        def columns(start, size):
            return pl.ds(pl.multiple_of(index * BLOCK + start, UNIT), size)

        apply_inverse(damping_ref[0, 0], rows_ref, columns, solved_ref, columns, scratch)
        return carry

    lax.fori_loop(0, width // BLOCK, one, 0)

    def compare(rows):
        product = dot(solved_ref[rows, :], rows_ref[...], (1, 1), None)
        right[rows] = product * left_ref[rows]

    by_rows(count, 256, compare)
    product = jnp.sum(right[...], axis=0, keepdims=True)
    term_ref[...] = jnp.sum(product, axis=1, keepdims=True)


VMEM = pl.BlockSpec(memory_space=pltpu.VMEM)
SMEM = pl.BlockSpec(memory_space=pltpu.SMEM)


def solve_act(damping, me, rows):
    count = rows.shape[0]
    return pl.pallas_call(
        act_kernel,
        out_shape=(jax.ShapeDtypeStruct((count, count), F32),)
        + tuple(jax.ShapeDtypeStruct((count, units * UNIT), BF16) for units, _, _ in MOVES),
        in_specs=[SMEM, SMEM, VMEM],
        out_specs=(VMEM,) * (len(MOVES) + 1),
        scratch_shapes=[pltpu.VMEM((count, BLOCK), BF16)] + solver_scratch(count),
        compiler_params=pltpu.CompilerParams(vmem_limit_bytes=ACT_MIB * 2**20),
        cost_estimate=pl.CostEstimate(
            flops=16 * 10**9, bytes_accessed=4 * 2**20, transcendentals=0
        ),
        name="solve_act",
    )(damping, me, rows)


def solve_grad(damping, rows, left):
    count, width = rows.shape
    return pl.pallas_call(
        grad_kernel,
        out_shape=(
            jax.ShapeDtypeStruct((count, width), BF16),
            jax.ShapeDtypeStruct((1, 1), F32),
        ),
        in_specs=[SMEM, VMEM, VMEM],
        out_specs=(VMEM, VMEM),
        scratch_shapes=[pltpu.VMEM((count, count), F32)] + solver_scratch(count),
        compiler_params=pltpu.CompilerParams(vmem_limit_bytes=GRAD_MIB * 2**20),
        cost_estimate=pl.CostEstimate(
            flops=45 * 10**9, bytes_accessed=8 * 2**20, transcendentals=0
        ),
        name="solve_grad",
    )(damping, rows, left)


def swap(value, offset):
    return lax.ppermute(value, "dp", [(i, i ^ offset) for i in range(8)])


def normalize_kernel(fwd_ref, bwd_ref, gain_ref, out_ref):
    gain = gain_ref[...]
    normed_b, _ = normalize(bwd_ref[...], gain)
    normed_f, _ = normalize(fwd_ref[...], gain)
    part = normed_f.shape[1] // out_ref.shape[0]
    for device in range(out_ref.shape[0]):
        if device in OWNERS:
            block = OWNERS.index(device)
            out_ref[device, :, :BLOCK] = normed_b[:, block * BLOCK : (block + 1) * BLOCK]
        else:
            out_ref[device, :, :BLOCK] = jnp.zeros((normed_b.shape[0], BLOCK), BF16)
        out_ref[device, :, BLOCK:] = normed_f[:, device * part : (device + 1) * part]


def forward_kernel(rows_ref, weight_ref, out_ref):
    for start in range(0, weight_ref.shape[1], 512):
        columns = slice(start, start + 512)
        forward = dot(rows_ref[:, BLOCK:], weight_ref[:, columns], precision=None)
        out_ref[:, columns] = forward.astype(BF16)


def product_kernel(me_ref, *refs):
    me = me_ref[0, 0]
    pieces, (forward_ref, weight_ref, gathered, out_ref) = refs[:-4], refs[-4:]
    groups, tokens, _ = out_ref.shape
    part, width = weight_ref.shape
    for offset, piece in enumerate(pieces):
        start = pl.multiple_of((me ^ offset) * tokens, tokens)
        gathered[pl.ds(start, tokens), :] = piece[...]
    for device in range(groups):
        out_ref[device, :, :width] = forward_ref[device * tokens : (device + 1) * tokens, :]
    backward = dot(gathered[...], weight_ref[...], (1, 1), None)
    out_ref[:, :, width:] = backward.astype(BF16).reshape(groups, tokens, part)


def finish_kernel(parts_ref, fwd_ref, bwd_ref, grad_ref, gain_ref, next_ref, back_ref):
    groups = parts_ref.shape[0]
    width = fwd_ref.shape[1]
    part = width // groups
    out_width = parts_ref.shape[2] - part

    def some(rows):
        for start in range(0, out_width, 1024):
            columns = slice(start, start + 1024)
            layer = parts_ref[0, rows, columns].astype(F32)
            for group in range(1, groups):
                layer += parts_ref[group, rows, columns].astype(F32)
            next_ref[0, rows, columns] = (fwd_ref[rows, columns].astype(F32) + layer).astype(BF16)
        next_ref[0, rows, out_width:] = fwd_ref[rows, out_width:]
        squares, inner = 0.0, 0.0
        for group in range(groups):
            columns = slice(group * part, (group + 1) * part)
            wide = bwd_ref[rows, columns].astype(F32)
            scaled = parts_ref[group, rows, out_width:].astype(F32) * gain_ref[:, columns]
            squares += jnp.sum(wide * wide, axis=1, keepdims=True)
            inner += jnp.sum(scaled * wide, axis=1, keepdims=True)
        scale = lax.rsqrt(squares * (1.0 / width) + EPS)
        pull = scale**3 * (inner * (1.0 / width))
        for group in range(groups):
            columns = slice(group * part, (group + 1) * part)
            wide = bwd_ref[rows, columns].astype(F32)
            scaled = parts_ref[group, rows, out_width:].astype(F32) * gain_ref[:, columns]
            out = grad_ref[rows, columns].astype(F32) + scale * scaled - wide * pull
            back_ref[0, rows, columns] = out.astype(BF16)

    by_rows(fwd_ref.shape[0], 16, some)


def update_kernel(entries, terms_ref, turned_ref, grad_ref, out_ref):
    terms = terms_ref[...]
    total = jnp.sum(jnp.sum(terms, axis=0, keepdims=True)[:, :1], axis=1, keepdims=True)
    ratio = jnp.sqrt(entries / total)
    out_ref[...] = (ratio * dot(turned_ref[...], grad_ref[...], precision=None)).astype(BF16)


def shape(*dims, dtype=BF16):
    return jax.ShapeDtypeStruct(dims, dtype)


def cost(flops, moved):
    return pl.CostEstimate(flops=flops, bytes_accessed=moved, transcendentals=0)


def params(mib):
    return pltpu.CompilerParams(vmem_limit_bytes=mib * 2**20)


def per_device(x_fwd, x_bwd, grad_in, gain, weight, damping):
    fwd = x_fwd[0]
    bwd = x_bwd[0]
    grad = grad_in[0]
    local_w = weight[0]
    tokens, width = fwd.shape
    own_rows, out_width = local_w.shape
    groups = lax.axis_size("dp")
    group = groups * tokens
    me = lax.axis_index("dp")
    me_value = me.reshape(1, 1)
    damp_value = damping.reshape(1, 1)

    upstream = grad[:, :out_width]
    other = swap(upstream, groups // 2)
    pieces = [upstream] + [swap(upstream, offset) for offset in range(1, groups // 2)]
    fwd_late, bwd_late, other = lax.optimization_barrier((fwd, bwd, other))
    pieces += [other] + [swap(other, offset) for offset in range(1, groups // 2)]

    sent = pl.pallas_call(
        normalize_kernel,
        out_shape=shape(groups, tokens, BLOCK + own_rows),
        in_specs=[VMEM] * 3,
        out_specs=VMEM,
        compiler_params=params(8),
        cost_estimate=cost(10**7, 3 * 10**6),
        name="normalize",
    )(fwd_late, bwd_late, gain)
    rows = lax.all_to_all(sent, "dp", 0, 0, tiled=True).reshape(group, BLOCK + own_rows)

    left, *moves = solve_act(damp_value, me_value, rows)

    forward = pl.pallas_call(
        forward_kernel,
        out_shape=shape(group, out_width),
        in_specs=[VMEM] * 2,
        out_specs=VMEM,
        compiler_params=params(12),
        cost_estimate=cost(2 * 10**9, 8 * 10**6),
        name="forward",
    )(rows, local_w)

    ready = lax.optimization_barrier((me_value, *pieces, forward, left))
    group_grad, products = pl.pallas_call(
        product_kernel,
        out_shape=(shape(group, out_width), shape(groups, tokens, out_width + own_rows)),
        in_specs=[SMEM] + [VMEM] * (len(pieces) + 2),
        out_specs=(VMEM,) * 2,
        compiler_params=params(16),
        cost_estimate=cost(4 * 10**9, 10**7),
        name="products",
    )(*ready[:-1], local_w)
    parts = lax.all_to_all(products, "dp", 0, 0, tiled=True)

    moves = moves[:1] + [
        lax.ppermute(piece, "dp", pairs) for piece, pairs in zip(moves[1:], PAIRS[1:])
    ]
    turned = pl.pallas_call(
        assemble_kernel,
        out_shape=shape(own_rows, group),
        in_specs=[SMEM] + [VMEM] * len(MOVES),
        out_specs=VMEM,
        scratch_shapes=[pltpu.VMEM((group, (2 * WINDOW + 2) * UNIT), BF16)],
        compiler_params=params(16),
        cost_estimate=cost(10**7, 3 * 10**6),
        name="assemble",
    )(me_value, *moves)

    grad_tilde, term = solve_grad(damp_value, group_grad, left)
    devices = lax.axis_size("section") * groups
    terms = lax.all_to_all(
        jnp.broadcast_to(term, (devices, 128)), ("section", "dp"), 0, 0, tiled=True
    )

    parts, _ = lax.optimization_barrier((parts, term))
    out_f, out_b = pl.pallas_call(
        finish_kernel,
        out_shape=(shape(1, tokens, width),) * 2,
        in_specs=[VMEM] * 5,
        out_specs=(VMEM,) * 2,
        compiler_params=params(12),
        cost_estimate=cost(10**7, 8 * 10**6),
        name="finish",
    )(parts, fwd, bwd, grad, gain)
    next_fwd = from_behind(out_f, "section", 1)
    next_grad = from_behind(out_b, "section", -1)
    terms, next_fwd, next_grad = lax.optimization_barrier((terms, next_fwd, next_grad))

    columns = 512
    entries = float(lax.axis_size("section") * width * out_width)
    update = pl.pallas_call(
        lambda *refs: update_kernel(entries, *refs),
        grid=(out_width // columns,),
        out_shape=shape(own_rows, out_width),
        in_specs=[
            pl.BlockSpec((devices, 128), lambda i: (0, 0)),
            pl.BlockSpec((own_rows, group), lambda i: (0, 0)),
            pl.BlockSpec((group, columns), lambda i: (0, i)),
        ],
        out_specs=pl.BlockSpec((own_rows, columns), lambda i: (0, i)),
        compiler_params=params(12),
        cost_estimate=cost(2 * 10**9, 8 * 10**6),
        name="update",
    )(terms, turned, grad_tilde)
    return (next_fwd, next_grad, update[None])


def solution(mesh):
    return jax.shard_map(
        per_device,
        mesh=mesh,
        in_specs=(
            P("section", "dp", None),
            P("section", "dp", None),
            P("section", "dp", None),
            P("section", None),
            P("section", "dp", None),
            P("section"),
        ),
        out_specs=(P("section", "dp", None), P("section", "dp", None), P("section", "dp", None)),
        check_vma=False,
    )
```

```python
import jax
import jax.numpy as jnp
from jax import lax
from jax.experimental import pallas as pl
from jax.experimental.pallas import tpu as pltpu
from jax.sharding import PartitionSpec as P

BLOCK = 1024
EPS = 1e-06
F32 = jnp.float32
BF16 = jnp.bfloat16
EXACT = lax.Precision.HIGHEST


def dot(a, b, contract=(1, 0), precision=EXACT):
    return lax.dot_general(
        a,
        b,
        (((contract[0],), (contract[1],)), ((), ())),
        precision=precision,
        preferred_element_type=F32,
    )


def from_behind(value, axis, steps):
    count = lax.axis_size(axis)
    leading, last = (max(0, -steps), min(count, count - steps))
    return lax.ppermute(value, axis, [(source, source + steps) for source in range(leading, last)])


def normalize(x, gain):
    wide = x.astype(F32)
    scale = lax.rsqrt(jnp.mean(wide * wide, axis=-1, keepdims=True) + EPS)
    return ((wide * scale * gain).astype(BF16), scale)


def eye_mask(order):
    rows = lax.broadcasted_iota(jnp.int32, (order, order), 0)
    return rows == lax.broadcasted_iota(jnp.int32, (order, order), 1)


def step_coefficients(low, high):
    mid, half = (low + high) * 0.5, (high - low) * 0.5
    scale = 1.0 / (2.0 * mid * mid - half * half)
    return 4.0 * mid * scale, 2.0 * scale, half * half * scale


def split(value):
    high = value.astype(BF16)
    rest = value - high.astype(F32)
    middle = rest.astype(BF16)
    return high, middle, (rest - middle.astype(F32)).astype(BF16)


def dot_three(a, b):
    a_high, a_low, _ = split(a)
    b_high, b_low, _ = split(b)
    low = dot(a_low, b_high, precision=None) + dot(a_high, b_low, precision=None)
    return low + dot(a_high, b_high, precision=None)


def fourth_root(square):
    return jnp.sqrt(jnp.sqrt(jnp.sum(square * square)))


def by_rows(count, step, body):
    def one(index, carry):
        body(pl.ds(pl.multiple_of(index * step, step), step))
        return carry

    lax.fori_loop(0, count // step, one, 0)


def scaled_newton(spread, step):
    def once(spread):
        first, second, after = step_coefficients(1.0 - spread, 1.0 + spread)
        step(first, second)
        return after

    lax.while_loop(lambda spread: spread > 2e-2, once, spread)


def invert(matrix, low, state):
    order = matrix.shape[0]
    eye = eye_mask(order).astype(F32)
    square = dot(matrix, matrix)
    high = jnp.maximum(fourth_root(square), low) * 1.001
    first, second, spread = step_coefficients(low, high)
    state[:order] = first * eye - second * matrix
    state[order:] = first * matrix - second * square

    def step(first, second):
        both = state[...]
        state[...] = first * both - second * dot_three(both, both[order:])

    scaled_newton(spread, step)
    guess = state[:order]
    return guess + dot_three(guess, eye - dot(matrix, guess))


def invert_by_halves(factor, damping, state, parts):
    half = factor.shape[0] // 2
    parts[0] = factor[:half, :half]

    def stage(index, carry):
        inverse = invert(parts[index], damping, state)

        @pl.when(index == 0)
        def _():
            corner, upper = parts[0], factor[:half, half:]
            tall = dot(inverse, upper)

            parts[3] = tall - dot(inverse, dot(corner, tall) - upper)
            tall = parts[3]
            error = dot(corner, tall) - upper
            parts[1] = factor[half:, half:] - dot(tall.T, upper - error)

            parts[2] = inverse

        @pl.when(index == 1)
        def _():
            parts[1] = inverse

        return carry

    lax.fori_loop(0, 2, stage, 0)
    inverse, tall, rest = parts[2], parts[3], parts[1]
    cross = dot(tall, rest)
    factor[:half, :half] = inverse + dot(cross, tall.T)
    factor[:half, half:] = -cross
    factor[half:, :half] = -cross.T
    factor[half:, half:] = rest


def invert_whole(factor, damping, whole, spare):
    order = factor.shape[0]
    eye = eye_mask(order).astype(F32)

    def square(rows):
        spare[rows] = dot(factor[rows], factor[...])

    by_rows(order, 128, square)
    high = jnp.maximum(fourth_root(spare[...]), damping) * 1.001
    first, second, spread = step_coefficients(damping, high)
    whole[:order] = first * eye - second * factor[...]
    whole[order:] = first * factor[...] - second * spare[...]

    def step(first, second):
        spare[...] = whole[order:]

        def some(rows):
            whole[rows] = first * whole[rows] - second * dot(whole[rows], spare[...])

        by_rows(2 * order, 128, some)

    scaled_newton(spread, step)

    def polish(_, carry):
        def residual(rows):
            spare[rows] = dot(factor[rows], whole[:order])

        by_rows(order, 128, residual)
        spare[...] = eye - spare[...]

        def correct(rows):
            whole[rows] += dot(whole[rows], spare[...])

        by_rows(order, 128, correct)
        return carry

    lax.fori_loop(0, 3, polish, 0)


def apply_inverse(damping, rows_ref, columns, out_ref, out_columns, scratch):
    factor, state, parts, whole, spare = scratch
    count = rows_ref.shape[0]
    half = count // 2
    width = 256

    def gram(rows):
        factor[rows] = dot(rows_ref[rows, columns(0, BLOCK)], rows_ref[:, columns(0, BLOCK)], (1, 1), None) * (
            1.0 / count
        )

    by_rows(count, half, gram)
    squares = []
    for corner in (factor[:half, :half], factor[half:, half:]):
        corner = corner.astype(BF16)
        squares.append(jnp.abs(dot(corner, corner, precision=None)))
    easy = fourth_root(jnp.maximum(*squares)) < HARDEST * damping
    factor[...] = jnp.where(eye_mask(count), factor[...] + damping, factor[...])

    @pl.when(easy)
    def _():
        invert_by_halves(factor, damping, state, parts)

        def solve(rows):
            high, low, _ = split(factor[rows])
            block = rows_ref[:, columns(0, BLOCK)]
            solved = dot(low, block, precision=None) + dot(high, block, precision=None)
            out_ref[rows, out_columns(0, BLOCK)] = solved.astype(BF16)

        by_rows(count, half, solve)

    @pl.when(jnp.logical_not(easy))
    def _():
        invert_whole(factor, damping, whole, spare)

        def solve(index, carry):
            start = index * width
            exact = rows_ref[:, columns(start, width)].astype(F32)

            def guess(rows):
                spare[rows, :width] = dot(whole[rows], exact)

            def residual(rows):
                spare[rows, width:] = dot(factor[rows], spare[:, :width])

            def correct(rows):
                fixed = spare[rows, :width] + dot(whole[rows], spare[:, width:])
                out_ref[rows, out_columns(start, width)] = fixed.astype(BF16)

            by_rows(count, 128, guess)
            by_rows(count, 128, residual)
            spare[:, width:] = exact - spare[:, width:]
            by_rows(count, 128, correct)
            return carry

        lax.fori_loop(0, BLOCK // width, solve, 0)


HARDEST = 2e4


def solver_scratch(count):
    half = count // 2
    return [
        pltpu.VMEM((count, count), F32),
        pltpu.VMEM((count, half), F32),
        pltpu.VMEM((4, half, half), F32),
        pltpu.VMEM((2 * count, count), F32),
        pltpu.VMEM((count, count), F32),
    ]


OWNERS = (0, 2, 4, 5, 7)
UNIT = 128
MOVES = (
    (5, {0: 0, 2: 2, 4: 3, 5: 1, 7: 3}, {0: 0, 2: 0, 4: -1, 5: 0, 7: 0}),
    (4, {0: 4, 4: 0, 7: 0}, {1: -1, 3: 1, 6: 2}),
    (2, {2: 0, 5: 6}, {1: 3, 6: 0}),
    (1, {2: 7, 5: 0}, {3: 0, 4: 4}),
)
PAIRS = (None, ((0, 1), (4, 3), (7, 6)), ((2, 1), (5, 6)), ((2, 3), (5, 4)))
WINDOW = 5


def lookup(table, missing, me):
    value = jnp.int32(missing)
    for device, entry in table.items():
        value = jnp.where(me == device, entry, value)
    return value


def act_kernel(damping_ref, me_ref, rows_ref, left_ref, *refs):
    moves, (solved_ref, *scratch) = refs[: len(MOVES)], refs[len(MOVES) :]

    def columns(start, size):
        return slice(start, start + size) if isinstance(start, int) else pl.ds(start, size)

    apply_inverse(damping_ref[0, 0], rows_ref, columns, solved_ref, columns, scratch)

    def compare(rows):
        left_ref[rows] = dot(solved_ref[rows, :], rows_ref[:, :BLOCK], (1, 1), None)

    by_rows(solved_ref.shape[0], 256, compare)
    for (units, first, _), out in zip(MOVES, moves):
        start = pl.multiple_of(lookup(first, 0, me_ref[0, 0]) * UNIT, UNIT)
        out[...] = solved_ref[:, pl.ds(start, units * UNIT)]


def assemble_kernel(me_ref, *refs):
    moves, (out_ref, buffer) = refs[: len(MOVES)], refs[len(MOVES) :]
    for (units, _, place), piece in zip(MOVES, moves):
        start = (lookup(place, WINDOW + 1, me_ref[0, 0]) + 1) * UNIT
        buffer[:, pl.ds(pl.multiple_of(start, UNIT), units * UNIT)] = piece[...]
    out_ref[...] = buffer[:, UNIT : (WINDOW + 1) * UNIT].T


def grad_kernel(damping_ref, rows_ref, left_ref, solved_ref, term_ref, right, *scratch):
    count, width = rows_ref.shape

    def one(index, carry):
        def columns(start, size):
            return pl.ds(pl.multiple_of(index * BLOCK + start, UNIT), size)

        apply_inverse(damping_ref[0, 0], rows_ref, columns, solved_ref, columns, scratch)
        return carry

    lax.fori_loop(0, width // BLOCK, one, 0)

    def compare(rows):
        product = dot(solved_ref[rows, :], rows_ref[...], (1, 1), None)
        right[rows] = product * left_ref[rows]

    by_rows(count, 256, compare)
    product = jnp.sum(right[...], axis=0, keepdims=True)
    term_ref[...] = jnp.sum(product, axis=1, keepdims=True)


SMEM = pl.BlockSpec(memory_space=pltpu.SMEM)


def shape(*dims, dtype=BF16):
    return jax.ShapeDtypeStruct(dims, dtype)


def whole_block(value):
    return pl.BlockSpec(value.shape, lambda i: (0,) * len(value.shape))


def cost(flops, moved):
    return pl.CostEstimate(flops=flops, bytes_accessed=moved, transcendentals=0)


def params():
    return pltpu.CompilerParams(vmem_limit_bytes=56 * 2**20)


def run(kernel, name, outs, scalars, arrays, flops, scratch=()):
    moved = sum(value.size * value.dtype.itemsize for value in (*arrays, *outs))
    return pl.pallas_call(
        kernel,
        grid=(1,),
        out_shape=tuple(outs),
        in_specs=[SMEM] * len(scalars) + [whole_block(value) for value in arrays],
        out_specs=tuple(whole_block(value) for value in outs),
        scratch_shapes=list(scratch),
        compiler_params=params(),
        cost_estimate=cost(flops, moved),
        name=name,
    )(*scalars, *arrays)


def solve_act(damping, me, rows):
    count = rows.shape[0]
    outs = [shape(count, count, dtype=F32)]
    outs += [shape(count, units * UNIT) for units, _, _ in MOVES]
    scratch = [pltpu.VMEM((count, BLOCK), BF16)] + solver_scratch(count)
    return run(act_kernel, "solve_act", outs, (damping, me), (rows,), 16 * 10**9, scratch)


def solve_grad(damping, rows, left):
    count, width = rows.shape
    outs = [shape(count, width), shape(1, 1, dtype=F32)]
    scratch = [pltpu.VMEM((count, count), F32)] + solver_scratch(count)
    return run(grad_kernel, "solve_grad", outs, (damping,), (rows, left), 45 * 10**9, scratch)


def swap(value, offset):
    return lax.ppermute(value, "dp", [(i, i ^ offset) for i in range(8)])


def normalize_kernel(fwd_ref, bwd_ref, gain_ref, out_ref):
    gain = gain_ref[...]
    normed_b, _ = normalize(bwd_ref[...], gain)
    normed_f, _ = normalize(fwd_ref[...], gain)
    part = normed_f.shape[1] // out_ref.shape[0]
    for device in range(out_ref.shape[0]):
        if device in OWNERS:
            block = OWNERS.index(device)
            out_ref[device, :, :BLOCK] = normed_b[:, block * BLOCK : (block + 1) * BLOCK]
        else:
            out_ref[device, :, :BLOCK] = jnp.zeros((normed_b.shape[0], BLOCK), BF16)
        out_ref[device, :, BLOCK:] = normed_f[:, device * part : (device + 1) * part]


def forward_kernel(rows_ref, weight_ref, out_ref):
    for start in range(0, weight_ref.shape[1], 512):
        columns = slice(start, start + 512)
        forward = dot(rows_ref[:, BLOCK:], weight_ref[:, columns], precision=None)
        out_ref[:, columns] = forward.astype(BF16)


def product_kernel(me_ref, *refs):
    me = me_ref[0, 0]
    pieces, (forward_ref, weight_ref, gathered, out_ref) = refs[:-4], refs[-4:]
    groups, tokens, _ = out_ref.shape
    part, width = weight_ref.shape
    for offset, piece in enumerate(pieces):
        for half in range(2):
            start = pl.multiple_of((me ^ offset ^ (half * groups // 2)) * tokens, tokens)
            gathered[pl.ds(start, tokens), :] = piece[half * tokens : (half + 1) * tokens, :]
    for device in range(groups):
        out_ref[device, :, :width] = forward_ref[device * tokens : (device + 1) * tokens, :]
    backward = dot(gathered[...], weight_ref[...], (1, 1), None)
    out_ref[:, :, width:] = backward.astype(BF16).reshape(groups, tokens, part)


def finish_kernel(parts_ref, fwd_ref, bwd_ref, grad_ref, gain_ref, next_ref, back_ref):
    groups = parts_ref.shape[0]
    width = fwd_ref.shape[1]
    part = width // groups
    out_width = parts_ref.shape[2] - part

    def some(rows):
        for start in range(0, out_width, 1024):
            columns = slice(start, start + 1024)
            layer = parts_ref[0, rows, columns].astype(F32)
            for group in range(1, groups):
                layer += parts_ref[group, rows, columns].astype(F32)
            next_ref[0, rows, columns] = (fwd_ref[rows, columns].astype(F32) + layer).astype(BF16)
        next_ref[0, rows, out_width:] = fwd_ref[rows, out_width:]
        squares, inner = 0.0, 0.0
        for group in range(groups):
            columns = slice(group * part, (group + 1) * part)
            wide = bwd_ref[rows, columns].astype(F32)
            scaled = parts_ref[group, rows, out_width:].astype(F32) * gain_ref[:, columns]
            squares += jnp.sum(wide * wide, axis=1, keepdims=True)
            inner += jnp.sum(scaled * wide, axis=1, keepdims=True)
        scale = lax.rsqrt(squares * (1.0 / width) + EPS)
        pull = scale**3 * (inner * (1.0 / width))
        for group in range(groups):
            columns = slice(group * part, (group + 1) * part)
            wide = bwd_ref[rows, columns].astype(F32)
            scaled = parts_ref[group, rows, out_width:].astype(F32) * gain_ref[:, columns]
            out = grad_ref[rows, columns].astype(F32) + scale * scaled - wide * pull
            back_ref[0, rows, columns] = out.astype(BF16)

    by_rows(fwd_ref.shape[0], 16, some)


def update_kernel(
    entries, terms_ref, turned_ref, grad_ref, fwd_ref, back_ref, out_ref, next_ref, last_ref, sems
):
    copies = (
        pltpu.make_async_copy(fwd_ref, next_ref, sems.at[0]),
        pltpu.make_async_copy(back_ref, last_ref, sems.at[1]),
    )

    @pl.when(pl.program_id(0) == 0)
    def _():
        for copy in copies:
            copy.start()

    terms = terms_ref[...]
    total = jnp.sum(jnp.sum(terms, axis=0, keepdims=True)[:, :1], axis=1, keepdims=True)
    ratio = jnp.sqrt(entries / total)
    out_ref[...] = (ratio * dot(turned_ref[...], grad_ref[...], precision=None)).astype(BF16)

    @pl.when(pl.program_id(0) == pl.num_programs(0) - 1)
    def _():
        for copy in copies:
            copy.wait()


def per_device(x_fwd, x_bwd, grad_in, gain, weight, damping):
    fwd = x_fwd[0]
    bwd = x_bwd[0]
    grad = grad_in[0]
    local_w = weight[0]
    tokens, width = fwd.shape
    own_rows, out_width = local_w.shape
    groups = lax.axis_size("dp")
    group = groups * tokens
    me = lax.axis_index("dp")
    me_value = me.reshape(1, 1)
    damp_value = damping.reshape(1, 1)

    upstream = grad[:, :out_width]
    half = groups // 2
    other = swap(upstream, half)
    (sent,) = run(
        normalize_kernel,
        "normalize",
        [shape(groups, tokens, BLOCK + own_rows)],
        (),
        (fwd, bwd, gain),
        10**7,
    )
    sent, other = lax.optimization_barrier((sent, other))
    pair = jnp.concatenate([upstream, other], axis=0)
    pieces = [pair] + [swap(pair, offset) for offset in range(1, half)]
    rows = lax.all_to_all(sent, "dp", 0, 0, tiled=True).reshape(group, BLOCK + own_rows)

    left, *moves = solve_act(damp_value, me_value, rows)
    (forward,) = run(
        forward_kernel, "forward", [shape(group, out_width)], (), (rows, local_w), 2 * 10**9
    )
    ready = lax.optimization_barrier((me_value, *pieces, forward, left))
    group_grad, products = run(
        product_kernel,
        "products",
        [shape(group, out_width), shape(groups, tokens, out_width + own_rows)],
        ready[:1],
        (*ready[1:-1], local_w),
        2 * 10**9,
    )
    parts = lax.all_to_all(products, "dp", 0, 0, tiled=True)

    moves = moves[:1] + [
        lax.ppermute(piece, "dp", pairs) for piece, pairs in zip(moves[1:], PAIRS[1:])
    ]
    (turned,) = run(
        assemble_kernel,
        "assemble",
        [shape(own_rows, group)],
        (me_value,),
        moves,
        10**7,
        [pltpu.VMEM((group, (2 * WINDOW + 2) * UNIT), BF16)],
    )

    grad_tilde, term = solve_grad(damp_value, group_grad, left)
    devices = lax.axis_size("section") * groups
    terms = lax.all_to_all(
        jnp.broadcast_to(term, (devices, 128)), ("section", "dp"), 0, 0, tiled=True
    )

    parts, _ = lax.optimization_barrier((parts, term))
    out_f, out_b = run(
        finish_kernel,
        "finish",
        [shape(1, tokens, width)] * 2,
        (),
        (parts, fwd, bwd, grad, gain),
        10**7,
    )
    next_fwd = from_behind(out_f, "section", 1)
    next_grad = from_behind(out_b, "section", -1)
    terms, next_fwd, next_grad = lax.optimization_barrier((terms, next_fwd, next_grad))

    columns = 512
    entries = float(lax.axis_size("section") * width * out_width)
    keep = pl.BlockSpec(memory_space=pl.ANY)
    update, next_fwd, next_grad = pl.pallas_call(
        lambda *refs: update_kernel(entries, *refs),
        grid=(out_width // columns,),
        out_shape=(shape(own_rows, out_width),) + (shape(1, tokens, width),) * 2,
        in_specs=[
            pl.BlockSpec((devices, 128), lambda i: (0, 0)),
            pl.BlockSpec((own_rows, group), lambda i: (0, 0)),
            pl.BlockSpec((group, columns), lambda i: (0, i)),
            keep,
            keep,
        ],
        out_specs=(pl.BlockSpec((own_rows, columns), lambda i: (0, i)), keep, keep),
        scratch_shapes=[pltpu.SemaphoreType.DMA((2,))],
        compiler_params=params(),
        cost_estimate=cost(2 * 10**9, 8 * 10**6),
        name="update",
    )(terms, turned, grad_tilde, next_fwd, next_grad)
    return (next_fwd, next_grad, update[None])


def solution(mesh):
    return jax.shard_map(
        per_device,
        mesh=mesh,
        in_specs=(
            P("section", "dp", None),
            P("section", "dp", None),
            P("section", "dp", None),
            P("section", None),
            P("section", "dp", None),
            P("section"),
        ),
        out_specs=(P("section", "dp", None), P("section", "dp", None), P("section", "dp", None)),
        check_vma=False,
    )
```

```python
import jax
import jax.numpy as jnp
from jax import lax
from jax.experimental import pallas as pl
from jax.experimental.pallas import tpu as pltpu
from jax.sharding import PartitionSpec as P

BLOCK = 1024
EPS = 1e-06
F32 = jnp.float32
BF16 = jnp.bfloat16
EXACT = lax.Precision.HIGHEST


def dot(a, b, contract=(1, 0), precision=EXACT):
    return lax.dot_general(
        a,
        b,
        (((contract[0],), (contract[1],)), ((), ())),
        precision=precision,
        preferred_element_type=F32,
    )


def from_behind(value, axis, steps):
    count = lax.axis_size(axis)
    leading, last = (max(0, -steps), min(count, count - steps))
    return lax.ppermute(value, axis, [(source, source + steps) for source in range(leading, last)])


def normalize(x, gain):
    wide = x.astype(F32)
    scale = lax.rsqrt(jnp.mean(wide * wide, axis=-1, keepdims=True) + EPS)
    return ((wide * scale * gain).astype(BF16), scale)


def eye_mask(order):
    rows = lax.broadcasted_iota(jnp.int32, (order, order), 0)
    return rows == lax.broadcasted_iota(jnp.int32, (order, order), 1)


def step_coefficients(low, high):
    mid, half = (low + high) * 0.5, (high - low) * 0.5
    scale = 1.0 / (2.0 * mid * mid - half * half)
    return 4.0 * mid * scale, 2.0 * scale, half * half * scale


def split(value):
    high = value.astype(BF16)
    rest = value - high.astype(F32)
    middle = rest.astype(BF16)
    return high, middle, (rest - middle.astype(F32)).astype(BF16)


def dot_three(a, b):
    a_high, a_low, _ = split(a)
    b_high, b_low, _ = split(b)
    low = dot(a_low, b_high, precision=None) + dot(a_high, b_low, precision=None)
    return low + dot(a_high, b_high, precision=None)


def fourth_root(square):
    return jnp.sqrt(jnp.sqrt(jnp.sum(square * square)))


def by_rows(count, step, body):
    def one(index, carry):
        body(pl.ds(pl.multiple_of(index * step, step), step))
        return carry

    lax.fori_loop(0, count // step, one, 0)


def scaled_newton(spread, step):
    def once(spread):
        first, second, after = step_coefficients(1.0 - spread, 1.0 + spread)
        step(first, second)
        return after

    lax.while_loop(lambda spread: spread > 2e-2, once, spread)


def invert(matrix, low, state):
    order = matrix.shape[0]
    eye = eye_mask(order).astype(F32)
    square = dot(matrix, matrix)
    high = jnp.maximum(fourth_root(square), low) * 1.001
    first, second, spread = step_coefficients(low, high)
    state[:order] = first * eye - second * matrix
    state[order:] = first * matrix - second * square

    def step(first, second):
        both = state[...]
        state[...] = first * both - second * dot_three(both, both[order:])

    scaled_newton(spread, step)
    guess = state[:order]
    return guess + dot_three(guess, eye - dot(matrix, guess))


def invert_by_halves(factor, damping, state, parts):
    half = factor.shape[0] // 2
    parts[0] = factor[:half, :half]

    def stage(index, carry):
        inverse = invert(parts[index], damping, state)

        @pl.when(index == 0)
        def _():
            corner, upper = parts[0], factor[:half, half:]
            tall = dot(inverse, upper)

            parts[3] = tall - dot(inverse, dot(corner, tall) - upper)
            tall = parts[3]
            error = dot(corner, tall) - upper
            parts[1] = factor[half:, half:] - dot(tall.T, upper - error)

            parts[2] = inverse

        @pl.when(index == 1)
        def _():
            parts[1] = inverse

        return carry

    lax.fori_loop(0, 2, stage, 0)
    inverse, tall, rest = parts[2], parts[3], parts[1]
    cross = dot(tall, rest)
    factor[:half, :half] = inverse + dot(cross, tall.T)
    factor[:half, half:] = -cross
    factor[half:, :half] = -cross.T
    factor[half:, half:] = rest


def invert_whole(factor, damping, whole, spare):
    order = factor.shape[0]
    eye = eye_mask(order).astype(F32)

    def square(rows):
        spare[rows] = dot(factor[rows], factor[...])

    by_rows(order, 128, square)
    high = jnp.maximum(fourth_root(spare[...]), damping) * 1.001
    first, second, spread = step_coefficients(damping, high)
    whole[:order] = first * eye - second * factor[...]
    whole[order:] = first * factor[...] - second * spare[...]

    def step(first, second):
        spare[...] = whole[order:]

        def some(rows):
            whole[rows] = first * whole[rows] - second * dot(whole[rows], spare[...])

        by_rows(2 * order, 128, some)

    scaled_newton(spread, step)

    def polish(_, carry):
        def residual(rows):
            spare[rows] = dot(factor[rows], whole[:order])

        by_rows(order, 128, residual)
        spare[...] = eye - spare[...]

        def correct(rows):
            whole[rows] += dot(whole[rows], spare[...])

        by_rows(order, 128, correct)
        return carry

    lax.fori_loop(0, 3, polish, 0)


def apply_inverse(damping, rows_ref, columns, out_ref, out_columns, scratch):
    factor, state, parts, whole, spare = scratch
    count = rows_ref.shape[0]
    half = count // 2
    width = 256

    def gram(rows):
        factor[rows] = dot(rows_ref[rows, columns(0, BLOCK)], rows_ref[:, columns(0, BLOCK)], (1, 1), None) * (
            1.0 / count
        )

    by_rows(count, half, gram)
    squares = []
    for corner in (factor[:half, :half], factor[half:, half:]):
        corner = corner.astype(BF16)
        squares.append(jnp.abs(dot(corner, corner, precision=None)))
    easy = fourth_root(jnp.maximum(*squares)) < HARDEST * damping
    factor[...] = jnp.where(eye_mask(count), factor[...] + damping, factor[...])

    @pl.when(easy)
    def _():
        invert_by_halves(factor, damping, state, parts)

        def solve(rows):
            high, low, _ = split(factor[rows])
            block = rows_ref[:, columns(0, BLOCK)]
            solved = dot(low, block, precision=None) + dot(high, block, precision=None)
            out_ref[rows, out_columns(0, BLOCK)] = solved.astype(BF16)

        by_rows(count, half, solve)

    @pl.when(jnp.logical_not(easy))
    def _():
        invert_whole(factor, damping, whole, spare)

        def solve(index, carry):
            start = index * width
            exact = rows_ref[:, columns(start, width)].astype(F32)

            def guess(rows):
                spare[rows, :width] = dot(whole[rows], exact)

            def residual(rows):
                spare[rows, width:] = dot(factor[rows], spare[:, :width])

            def correct(rows):
                fixed = spare[rows, :width] + dot(whole[rows], spare[:, width:])
                out_ref[rows, out_columns(start, width)] = fixed.astype(BF16)

            by_rows(count, 128, guess)
            by_rows(count, 128, residual)
            spare[:, width:] = exact - spare[:, width:]
            by_rows(count, 128, correct)
            return carry

        lax.fori_loop(0, BLOCK // width, solve, 0)


HARDEST = 2e4


def solver_scratch(count):
    half = count // 2
    return [
        pltpu.VMEM((count, count), F32),
        pltpu.VMEM((count, half), F32),
        pltpu.VMEM((4, half, half), F32),
        pltpu.VMEM((2 * count, count), F32),
        pltpu.VMEM((count, count), F32),
    ]


OWNERS = (0, 2, 4, 5, 7)
UNIT = 128
MOVES = (
    (5, {0: 0, 2: 2, 4: 3, 5: 1, 7: 3}, {0: 0, 2: 0, 4: -1, 5: 0, 7: 0}),
    (4, {0: 4, 4: 0, 7: 0}, {1: -1, 3: 1, 6: 2}),
    (2, {2: 0, 5: 6}, {1: 3, 6: 0}),
    (1, {2: 7, 5: 0}, {3: 0, 4: 4}),
)
PAIRS = (None, ((0, 1), (4, 3), (7, 6)), ((2, 1), (5, 6)), ((2, 3), (5, 4)))
WINDOW = 5


def lookup(table, missing, me):
    value = jnp.int32(missing)
    for device, entry in table.items():
        value = jnp.where(me == device, entry, value)
    return value


def act_kernel(damping_ref, me_ref, rows_ref, left_ref, *refs):
    moves, (solved_ref, *scratch) = refs[: len(MOVES)], refs[len(MOVES) :]

    def columns(start, size):
        return slice(start, start + size) if isinstance(start, int) else pl.ds(start, size)

    apply_inverse(damping_ref[0, 0], rows_ref, columns, solved_ref, columns, scratch)

    def compare(rows):
        left_ref[rows] = dot(solved_ref[rows, :], rows_ref[:, :BLOCK], (1, 1), None)

    by_rows(solved_ref.shape[0], 256, compare)
    for (units, first, _), out in zip(MOVES, moves):
        start = pl.multiple_of(lookup(first, 0, me_ref[0, 0]) * UNIT, UNIT)
        out[...] = solved_ref[:, pl.ds(start, units * UNIT)]


def assemble_kernel(me_ref, *refs):
    moves, (out_ref, buffer) = refs[: len(MOVES)], refs[len(MOVES) :]
    for (units, _, place), piece in zip(MOVES, moves):
        start = (lookup(place, WINDOW + 1, me_ref[0, 0]) + 1) * UNIT
        buffer[:, pl.ds(pl.multiple_of(start, UNIT), units * UNIT)] = piece[...]
    out_ref[...] = buffer[:, UNIT : (WINDOW + 1) * UNIT].T


def grad_kernel(damping_ref, rows_ref, left_ref, solved_ref, term_ref, right, *scratch):
    count, width = rows_ref.shape

    def one(index, carry):
        def columns(start, size):
            return pl.ds(pl.multiple_of(index * BLOCK + start, UNIT), size)

        apply_inverse(damping_ref[0, 0], rows_ref, columns, solved_ref, columns, scratch)
        return carry

    lax.fori_loop(0, width // BLOCK, one, 0)

    def compare(rows):
        product = dot(solved_ref[rows, :], rows_ref[...], (1, 1), None)
        right[rows] = product * left_ref[rows]

    by_rows(count, 256, compare)
    product = jnp.sum(right[...], axis=0, keepdims=True)
    term_ref[...] = jnp.sum(product, axis=1, keepdims=True)


SMEM = pl.BlockSpec(memory_space=pltpu.SMEM)


def shape(*dims, dtype=BF16):
    return jax.ShapeDtypeStruct(dims, dtype)


def whole_block(value):
    return pl.BlockSpec(value.shape, lambda i: (0,) * len(value.shape))


def cost(flops, moved):
    return pl.CostEstimate(flops=flops, bytes_accessed=moved, transcendentals=0)


def params():
    return pltpu.CompilerParams(vmem_limit_bytes=56 * 2**20)


def run(kernel, name, outs, scalars, arrays, flops, scratch=()):
    moved = sum(value.size * value.dtype.itemsize for value in (*arrays, *outs))
    return pl.pallas_call(
        kernel,
        grid=(1,),
        out_shape=tuple(outs),
        in_specs=[SMEM] * len(scalars) + [whole_block(value) for value in arrays],
        out_specs=tuple(whole_block(value) for value in outs),
        scratch_shapes=list(scratch),
        compiler_params=params(),
        cost_estimate=cost(flops, moved),
        name=name,
    )(*scalars, *arrays)


def solve_act(damping, me, rows):
    count = rows.shape[0]
    outs = [shape(count, count, dtype=F32)]
    outs += [shape(count, units * UNIT) for units, _, _ in MOVES]
    scratch = [pltpu.VMEM((count, BLOCK), BF16)] + solver_scratch(count)
    return run(act_kernel, "solve_act", outs, (damping, me), (rows,), 16 * 10**9, scratch)


def solve_grad(damping, rows, left):
    count, width = rows.shape
    outs = [shape(count, width), shape(1, 1, dtype=F32)]
    scratch = [pltpu.VMEM((count, count), F32)] + solver_scratch(count)
    return run(grad_kernel, "solve_grad", outs, (damping,), (rows, left), 45 * 10**9, scratch)


def swap(value, offset):
    return lax.ppermute(value, "dp", [(i, i ^ offset) for i in range(8)])


def normalize_kernel(fwd_ref, bwd_ref, gain_ref, out_ref):
    gain = gain_ref[...]
    normed_b, _ = normalize(bwd_ref[...], gain)
    normed_f, _ = normalize(fwd_ref[...], gain)
    part = normed_f.shape[1] // out_ref.shape[0]
    for device in range(out_ref.shape[0]):
        if device in OWNERS:
            block = OWNERS.index(device)
            out_ref[device, :, :BLOCK] = normed_b[:, block * BLOCK : (block + 1) * BLOCK]
        else:
            out_ref[device, :, :BLOCK] = jnp.zeros((normed_b.shape[0], BLOCK), BF16)
        out_ref[device, :, BLOCK:] = normed_f[:, device * part : (device + 1) * part]


def forward_kernel(rows_ref, weight_ref, out_ref):
    forward = dot(rows_ref[:, BLOCK:], weight_ref[...], precision=None)
    out_ref[...] = forward.astype(BF16).reshape(out_ref.shape)


HELD = ((0, 4), (1, 5), (3, 7), (2,), (6,))


def product_kernel(me_ref, *refs):
    me = me_ref[0, 0]
    pieces, (weight_ref, _, gathered, out_ref, back, sem) = refs[: len(HELD)], refs[len(HELD) :]
    groups, tokens, part = back.shape
    for held, piece in zip(HELD, pieces):
        for index, offset in enumerate(held):
            start = pl.multiple_of((me ^ offset) * tokens, tokens)
            gathered[pl.ds(start, tokens), :] = piece[index * tokens : (index + 1) * tokens, :]
    backward = dot(gathered[...], weight_ref[...], (1, 1), None)
    back[...] = backward.astype(BF16).reshape(groups, tokens, part)
    copy = pltpu.make_async_copy(back, out_ref.at[:, :, pl.ds(weight_ref.shape[1], part)], sem)
    copy.start()
    copy.wait()


def finish_kernel(parts_ref, fwd_ref, bwd_ref, grad_ref, gain_ref, next_ref, back_ref):
    groups = parts_ref.shape[0]
    width = fwd_ref.shape[1]
    part = width // groups
    out_width = parts_ref.shape[2] - part

    rows = slice(None)
    for start in range(0, out_width, 1024):
        columns = slice(start, start + 1024)
        layer = parts_ref[0, rows, columns].astype(F32)
        for group in range(1, groups):
            layer += parts_ref[group, rows, columns].astype(F32)
        next_ref[0, rows, columns] = (fwd_ref[rows, columns].astype(F32) + layer).astype(BF16)
    next_ref[0, rows, out_width:] = fwd_ref[rows, out_width:]
    squares, inner = 0.0, 0.0
    for group in range(groups):
        columns = slice(group * part, (group + 1) * part)
        wide = bwd_ref[rows, columns].astype(F32)
        scaled = parts_ref[group, rows, out_width:].astype(F32) * gain_ref[:, columns]
        squares += jnp.sum(wide * wide, axis=1, keepdims=True)
        inner += jnp.sum(scaled * wide, axis=1, keepdims=True)
    scale = lax.rsqrt(squares * (1.0 / width) + EPS)
    pull = scale**3 * (inner * (1.0 / width))
    for group in range(groups):
        columns = slice(group * part, (group + 1) * part)
        wide = bwd_ref[rows, columns].astype(F32)
        scaled = parts_ref[group, rows, out_width:].astype(F32) * gain_ref[:, columns]
        out = grad_ref[rows, columns].astype(F32) + scale * scaled - wide * pull
        back_ref[0, rows, columns] = out.astype(BF16)


def update_kernel(
    entries, terms_ref, turned_ref, grad_ref, fwd_ref, back_ref, out_ref, next_ref, last_ref
):
    terms = terms_ref[...]
    total = jnp.sum(jnp.sum(terms, axis=0, keepdims=True)[:, :1], axis=1, keepdims=True)
    ratio = jnp.sqrt(entries / total)
    out_ref[...] = (ratio * dot(turned_ref[...], grad_ref[...], precision=None)).astype(BF16)
    next_ref[...] = fwd_ref[...]
    last_ref[...] = back_ref[...]


def per_device(x_fwd, x_bwd, grad_in, gain, weight, damping):
    fwd = x_fwd[0]
    bwd = x_bwd[0]
    grad = grad_in[0]
    local_w = weight[0]
    tokens, width = fwd.shape
    own_rows, out_width = local_w.shape
    groups = lax.axis_size("dp")
    group = groups * tokens
    me = lax.axis_index("dp")
    me_value = me.reshape(1, 1)
    damp_value = damping.reshape(1, 1)

    upstream = grad[:, :out_width]
    half = groups // 2
    other = swap(upstream, half)
    (sent,) = run(
        normalize_kernel,
        "normalize",
        [shape(groups, tokens, BLOCK + own_rows)],
        (),
        (fwd, bwd, gain),
        10**7,
    )
    sent, other = lax.optimization_barrier((sent, other))
    pair = jnp.concatenate([upstream, other], axis=0)
    near, far = swap(pair, 1), swap(pair, half - 1)
    rows = lax.all_to_all(sent, "dp", 0, 0, tiled=True).reshape(group, BLOCK + own_rows)

    left, *moves = solve_act(damp_value, me_value, rows)
    near, far, _ = lax.optimization_barrier((near, far, left))
    pieces = [pair, near, far, swap(far[:tokens], 1), swap(near[tokens:], half - 1)]
    columns = 512
    forward = pl.pallas_call(
        forward_kernel,
        grid=(out_width // columns,),
        out_shape=shape(groups, tokens, out_width + own_rows),
        in_specs=[
            pl.BlockSpec((group, BLOCK + own_rows), lambda i: (0, 0)),
            pl.BlockSpec((own_rows, columns), lambda i: (0, i)),
        ],
        out_specs=pl.BlockSpec((groups, tokens, columns), lambda i: (0, 0, i)),
        compiler_params=params(),
        cost_estimate=cost(2 * 10**9, 8 * 10**6),
        name="forward",
    )(rows, local_w)
    scalar, *arrays = lax.optimization_barrier((me_value, *pieces, forward, left))[:-1]
    arrays = arrays[:-1] + [local_w, arrays[-1]]
    keep = pl.BlockSpec(memory_space=pl.ANY)
    outs = (shape(group, out_width), shape(groups, tokens, out_width + own_rows))
    group_grad, products = pl.pallas_call(
        product_kernel,
        grid=(1,),
        out_shape=outs,
        in_specs=[SMEM] + [whole_block(value) for value in arrays[:-1]] + [keep],
        out_specs=(whole_block(outs[0]), keep),
        scratch_shapes=[
            pltpu.VMEM((groups, tokens, own_rows), BF16),
            pltpu.SemaphoreType.DMA,
        ],
        input_output_aliases={len(arrays): 1},
        compiler_params=params(),
        cost_estimate=cost(2 * 10**9, 10**7),
        name="products",
    )(scalar, *arrays)
    parts = lax.all_to_all(products, "dp", 0, 0, tiled=True)

    moves = moves[:1] + [
        lax.ppermute(piece, "dp", pairs) for piece, pairs in zip(moves[1:], PAIRS[1:])
    ]
    (turned,) = run(
        assemble_kernel,
        "assemble",
        [shape(own_rows, group)],
        (me_value,),
        moves,
        10**7,
        [pltpu.VMEM((group, (2 * WINDOW + 2) * UNIT), BF16)],
    )

    grad_tilde, term = solve_grad(damp_value, group_grad, left)
    devices = lax.axis_size("section") * groups
    terms = lax.all_to_all(
        jnp.broadcast_to(term, (devices, 128)), ("section", "dp"), 0, 0, tiled=True
    )

    parts, _ = lax.optimization_barrier((parts, term))
    step = 16
    wide_block = pl.BlockSpec((step, width), lambda i: (i, 0))
    out_block = pl.BlockSpec((1, step, width), lambda i: (0, i, 0))
    out_f, out_b = pl.pallas_call(
        finish_kernel,
        grid=(tokens // step,),
        out_shape=(shape(1, tokens, width),) * 2,
        in_specs=[
            pl.BlockSpec((groups, step, out_width + own_rows), lambda i: (0, i, 0)),
            wide_block,
            wide_block,
            wide_block,
            pl.BlockSpec((1, width), lambda i: (0, 0)),
        ],
        out_specs=(out_block, out_block),
        compiler_params=params(),
        cost_estimate=cost(10**7, 8 * 10**6),
        name="finish",
    )(parts, fwd, bwd, grad, gain)
    next_fwd = from_behind(out_f, "section", 1)
    next_grad = from_behind(out_b, "section", -1)
    terms, next_fwd, next_grad = lax.optimization_barrier((terms, next_fwd, next_grad))

    entries = float(lax.axis_size("section") * width * out_width)
    steps = 4
    columns = out_width // steps
    same = pl.BlockSpec((1, tokens, width // steps), lambda i: (0, 0, i))
    update, next_fwd, next_grad = pl.pallas_call(
        lambda *refs: update_kernel(entries, *refs),
        grid=(steps,),
        out_shape=(shape(own_rows, out_width),) + (shape(1, tokens, width),) * 2,
        in_specs=[
            pl.BlockSpec((devices, 128), lambda i: (0, 0)),
            pl.BlockSpec((own_rows, group), lambda i: (0, 0)),
            pl.BlockSpec((group, columns), lambda i: (0, i)),
            same,
            same,
        ],
        out_specs=(pl.BlockSpec((own_rows, columns), lambda i: (0, i)), same, same),
        compiler_params=params(),
        cost_estimate=cost(2 * 10**9, 8 * 10**6),
        name="update",
    )(terms, turned, grad_tilde, next_fwd, next_grad)
    return (next_fwd, next_grad, update[None])


def solution(mesh):
    return jax.shard_map(
        per_device,
        mesh=mesh,
        in_specs=(
            P("section", "dp", None),
            P("section", "dp", None),
            P("section", "dp", None),
            P("section", None),
            P("section", "dp", None),
            P("section"),
        ),
        out_specs=(P("section", "dp", None), P("section", "dp", None), P("section", "dp", None)),
        check_vma=False,
    )
```

```python
import jax
import jax.numpy as jnp
from jax import lax
from jax.experimental import pallas as pl
from jax.experimental.pallas import tpu as pltpu
from jax.sharding import PartitionSpec as P

BLOCK = 1024
EPS = 1e-06
F32 = jnp.float32
BF16 = jnp.bfloat16
EXACT = lax.Precision.HIGHEST


def dot(a, b, contract=(1, 0), precision=EXACT):
    return lax.dot_general(
        a,
        b,
        (((contract[0],), (contract[1],)), ((), ())),
        precision=precision,
        preferred_element_type=F32,
    )


def from_behind(value, axis, steps):
    count = lax.axis_size(axis)
    leading, last = (max(0, -steps), min(count, count - steps))
    return lax.ppermute(value, axis, [(source, source + steps) for source in range(leading, last)])


def normalize(x, gain):
    wide = x.astype(F32)
    scale = lax.rsqrt(jnp.mean(wide * wide, axis=-1, keepdims=True) + EPS)
    return ((wide * scale * gain).astype(BF16), scale)


def eye_mask(order):
    rows = lax.broadcasted_iota(jnp.int32, (order, order), 0)
    return rows == lax.broadcasted_iota(jnp.int32, (order, order), 1)


def step_coefficients(low, high):
    mid, half = (low + high) * 0.5, (high - low) * 0.5
    scale = 1.0 / (2.0 * mid * mid - half * half)
    return 4.0 * mid * scale, 2.0 * scale, half * half * scale


def split(value):
    high = value.astype(BF16)
    rest = value - high.astype(F32)
    middle = rest.astype(BF16)
    return high, middle, (rest - middle.astype(F32)).astype(BF16)


def dot_three(a, b):
    a_high, a_low, _ = split(a)
    b_high, b_low, _ = split(b)
    low = dot(a_low, b_high, precision=None) + dot(a_high, b_low, precision=None)
    return low + dot(a_high, b_high, precision=None)


def fourth_root(square):
    return jnp.sqrt(jnp.sqrt(jnp.sum(square * square)))


def by_rows(count, step, body):
    def one(index, carry):
        body(pl.ds(pl.multiple_of(index * step, step), step))
        return carry

    lax.fori_loop(0, count // step, one, 0)


def scaled_newton(spread, step):
    def once(spread):
        first, second, after = step_coefficients(1.0 - spread, 1.0 + spread)
        step(first, second)
        return after

    lax.while_loop(lambda spread: spread > 2e-2, once, spread)


def invert(matrix, low, state):
    order = matrix.shape[0]
    eye = eye_mask(order).astype(F32)
    square = dot(matrix, matrix)
    high = jnp.maximum(fourth_root(square), low) * 1.001
    first, second, spread = step_coefficients(low, high)
    state[:order] = first * eye - second * matrix
    state[order:] = first * matrix - second * square

    def step(first, second):
        both = state[...]
        state[...] = first * both - second * dot_three(both, both[order:])

    scaled_newton(spread, step)
    guess = state[:order]
    return guess + dot_three(guess, eye - dot(matrix, guess))


def invert_by_halves(factor, damping, state, parts):
    half = factor.shape[0] // 2
    parts[0] = factor[:half, :half]

    def stage(index, carry):
        inverse = invert(parts[index], damping, state)

        @pl.when(index == 0)
        def _():
            corner, upper = parts[0], factor[:half, half:]
            tall = dot(inverse, upper)

            parts[3] = tall - dot(inverse, dot(corner, tall) - upper)
            tall = parts[3]
            error = dot(corner, tall) - upper
            parts[1] = factor[half:, half:] - dot(tall.T, upper - error)

            parts[2] = inverse

        @pl.when(index == 1)
        def _():
            parts[1] = inverse

        return carry

    lax.fori_loop(0, 2, stage, 0)
    inverse, tall, rest = parts[2], parts[3], parts[1]
    cross = dot(tall, rest)
    factor[:half, :half] = inverse + dot(cross, tall.T)
    factor[:half, half:] = -cross
    factor[half:, :half] = -cross.T
    factor[half:, half:] = rest


def invert_whole(factor, damping, whole, spare):
    order = factor.shape[0]
    eye = eye_mask(order).astype(F32)

    def square(rows):
        spare[rows] = dot(factor[rows], factor[...])

    by_rows(order, 128, square)
    high = jnp.maximum(fourth_root(spare[...]), damping) * 1.001
    first, second, spread = step_coefficients(damping, high)
    whole[:order] = first * eye - second * factor[...]
    whole[order:] = first * factor[...] - second * spare[...]

    def step(first, second):
        spare[...] = whole[order:]

        def some(rows):
            whole[rows] = first * whole[rows] - second * dot(whole[rows], spare[...])

        by_rows(2 * order, 128, some)

    scaled_newton(spread, step)

    def polish(_, carry):
        def residual(rows):
            spare[rows] = dot(factor[rows], whole[:order])

        by_rows(order, 128, residual)
        spare[...] = eye - spare[...]

        def correct(rows):
            whole[rows] += dot(whole[rows], spare[...])

        by_rows(order, 128, correct)
        return carry

    lax.fori_loop(0, 3, polish, 0)


def apply_inverse(damping, rows_ref, columns, out_ref, out_columns, scratch):
    factor, state, parts, whole, spare = scratch
    count = rows_ref.shape[0]
    half = count // 2
    width = 256

    def gram(rows):
        factor[rows] = dot(rows_ref[rows, columns(0, BLOCK)], rows_ref[:, columns(0, BLOCK)], (1, 1), None) * (
            1.0 / count
        )

    by_rows(count, half, gram)
    squares = []
    for corner in (factor[:half, :half], factor[half:, half:]):
        corner = corner.astype(BF16)
        squares.append(jnp.abs(dot(corner, corner, precision=None)))
    easy = fourth_root(jnp.maximum(*squares)) < HARDEST * damping
    factor[...] = jnp.where(eye_mask(count), factor[...] + damping, factor[...])

    @pl.when(easy)
    def _():
        invert_by_halves(factor, damping, state, parts)

        def solve(rows):
            high, low, _ = split(factor[rows])
            block = rows_ref[:, columns(0, BLOCK)]
            solved = dot(low, block, precision=None) + dot(high, block, precision=None)
            out_ref[rows, out_columns(0, BLOCK)] = solved.astype(BF16)

        by_rows(count, half, solve)

    @pl.when(jnp.logical_not(easy))
    def _():
        invert_whole(factor, damping, whole, spare)

        def solve(index, carry):
            start = index * width
            exact = rows_ref[:, columns(start, width)].astype(F32)

            def guess(rows):
                spare[rows, :width] = dot(whole[rows], exact)

            def residual(rows):
                spare[rows, width:] = dot(factor[rows], spare[:, :width])

            def correct(rows):
                fixed = spare[rows, :width] + dot(whole[rows], spare[:, width:])
                out_ref[rows, out_columns(start, width)] = fixed.astype(BF16)

            by_rows(count, 128, guess)
            by_rows(count, 128, residual)
            spare[:, width:] = exact - spare[:, width:]
            by_rows(count, 128, correct)
            return carry

        lax.fori_loop(0, BLOCK // width, solve, 0)


HARDEST = 2e4


def solver_scratch(count):
    half = count // 2
    return [
        pltpu.VMEM((count, count), F32),
        pltpu.VMEM((count, half), F32),
        pltpu.VMEM((4, half, half), F32),
        pltpu.VMEM((2 * count, count), F32),
        pltpu.VMEM((count, count), F32),
    ]


OWNERS = (0, 2, 4, 5, 7)
UNIT = 128
MOVES = (
    (5, {0: 0, 2: 2, 4: 3, 5: 1, 7: 3}, {0: 0, 2: 0, 4: -1, 5: 0, 7: 0}),
    (4, {0: 4, 4: 0, 7: 0}, {1: -1, 3: 1, 6: 2}),
    (2, {2: 0, 5: 6}, {1: 3, 6: 0}),
    (1, {2: 7, 5: 0}, {3: 0, 4: 4}),
)
PAIRS = (None, ((0, 1), (4, 3), (7, 6)), ((2, 1), (5, 6)), ((2, 3), (5, 4)))
WINDOW = 5


def lookup(table, missing, me):
    value = jnp.int32(missing)
    for device, entry in table.items():
        value = jnp.where(me == device, entry, value)
    return value


def act_kernel(damping_ref, me_ref, rows_ref, left_ref, *refs):
    moves, (solved_ref, *scratch) = refs[: len(MOVES)], refs[len(MOVES) :]

    def columns(start, size):
        return slice(start, start + size) if isinstance(start, int) else pl.ds(start, size)

    apply_inverse(damping_ref[0, 0], rows_ref, columns, solved_ref, columns, scratch)

    def compare(rows):
        left_ref[rows] = dot(solved_ref[rows, :], rows_ref[:, :BLOCK], (1, 1), None)

    by_rows(solved_ref.shape[0], 256, compare)
    for (units, first, _), out in zip(MOVES, moves):
        start = pl.multiple_of(lookup(first, 0, me_ref[0, 0]) * UNIT, UNIT)
        out[...] = solved_ref[:, pl.ds(start, units * UNIT)]


def assemble_kernel(me_ref, *refs):
    moves, (out_ref, buffer) = refs[: len(MOVES)], refs[len(MOVES) :]
    for (units, _, place), piece in zip(MOVES, moves):
        start = (lookup(place, WINDOW + 1, me_ref[0, 0]) + 1) * UNIT
        buffer[:, pl.ds(pl.multiple_of(start, UNIT), units * UNIT)] = piece[...]
    out_ref[...] = buffer[:, UNIT : (WINDOW + 1) * UNIT].T


def grad_kernel(damping_ref, rows_ref, left_ref, solved_ref, term_ref, right, *scratch):
    count, width = rows_ref.shape

    def one(index, carry):
        def columns(start, size):
            return pl.ds(pl.multiple_of(index * BLOCK + start, UNIT), size)

        apply_inverse(damping_ref[0, 0], rows_ref, columns, solved_ref, columns, scratch)
        return carry

    lax.fori_loop(0, width // BLOCK, one, 0)

    def compare(rows):
        product = dot(solved_ref[rows, :], rows_ref[...], (1, 1), None)
        right[rows] = product * left_ref[rows]

    by_rows(count, 256, compare)
    product = jnp.sum(right[...], axis=0, keepdims=True)
    term_ref[...] = jnp.sum(product, axis=1, keepdims=True)


SMEM = pl.BlockSpec(memory_space=pltpu.SMEM)
VMEM = pl.BlockSpec(memory_space=pltpu.VMEM)


def shape(*dims, dtype=BF16):
    return jax.ShapeDtypeStruct(dims, dtype)


def whole_block(value):
    return pl.BlockSpec(value.shape, lambda i: (0,) * len(value.shape))


def cost(flops, moved):
    return pl.CostEstimate(flops=flops, bytes_accessed=moved, transcendentals=0)


def params(mib=56):
    return pltpu.CompilerParams(vmem_limit_bytes=mib * 2**20)


def run(kernel, name, outs, scalars, arrays, flops, scratch=(), mib=56):
    moved = sum(value.size * value.dtype.itemsize for value in (*arrays, *outs))
    return pl.pallas_call(
        kernel,
        grid=(1,),
        out_shape=tuple(outs),
        in_specs=[SMEM] * len(scalars) + [whole_block(value) for value in arrays],
        out_specs=tuple(whole_block(value) for value in outs),
        scratch_shapes=list(scratch),
        compiler_params=params(mib),
        cost_estimate=cost(flops, moved),
        name=name,
    )(*scalars, *arrays)


def solve_act(damping, me, rows):
    count = rows.shape[0]
    outs = [shape(count, count, dtype=F32)]
    outs += [shape(count, units * UNIT) for units, _, _ in MOVES]
    scratch = [pltpu.VMEM((count, BLOCK), BF16)] + solver_scratch(count)
    return run(act_kernel, "solve_act", outs, (damping, me), (rows,), 16 * 10**9, scratch, 28)


def solve_grad(damping, rows, left):
    count, width = rows.shape
    outs = [shape(count, width), shape(1, 1, dtype=F32)]
    scratch = [pltpu.VMEM((count, count), F32)] + solver_scratch(count)
    return run(grad_kernel, "solve_grad", outs, (damping,), (rows, left), 45 * 10**9, scratch)


def swap(value, offset):
    return lax.ppermute(value, "dp", [(i, i ^ offset) for i in range(8)])


def normalize_kernel(fwd_ref, bwd_ref, gain_ref, out_ref):
    gain = gain_ref[...]
    normed_b, _ = normalize(bwd_ref[...], gain)
    normed_f, _ = normalize(fwd_ref[...], gain)
    part = normed_f.shape[1] // out_ref.shape[0]
    for device in range(out_ref.shape[0]):
        if device in OWNERS:
            block = OWNERS.index(device)
            out_ref[device, :, :BLOCK] = normed_b[:, block * BLOCK : (block + 1) * BLOCK]
        else:
            out_ref[device, :, :BLOCK] = jnp.zeros((normed_b.shape[0], BLOCK), BF16)
        out_ref[device, :, BLOCK:] = normed_f[:, device * part : (device + 1) * part]


def forward_kernel(rows_ref, weight_ref, out_ref):
    width = out_ref.shape[2]
    columns = pl.ds(pl.multiple_of(pl.program_id(0) * width, width), width)
    forward = dot(rows_ref[:, BLOCK:], weight_ref[:, columns], precision=None)
    out_ref[...] = forward.astype(BF16).reshape(out_ref.shape)


HELD = ((0, 4), (1, 5), (3, 7), (2,), (6,))


def product_kernel(me_ref, *refs):
    me = me_ref[0, 0]
    pieces, (weight_ref, _, gathered, out_ref, back, sem) = refs[: len(HELD)], refs[len(HELD) :]
    groups, tokens, part = back.shape
    for held, piece in zip(HELD, pieces):
        for index, offset in enumerate(held):
            start = pl.multiple_of((me ^ offset) * tokens, tokens)
            gathered[pl.ds(start, tokens), :] = piece[index * tokens : (index + 1) * tokens, :]
    backward = dot(gathered[...], weight_ref[...], (1, 1), None)
    back[...] = backward.astype(BF16).reshape(groups, tokens, part)
    copy = pltpu.make_async_copy(back, out_ref.at[:, :, pl.ds(weight_ref.shape[1], part)], sem)
    copy.start()
    copy.wait()


def finish_kernel(parts_ref, fwd_ref, bwd_ref, grad_ref, gain_ref, next_ref, back_ref):
    groups = parts_ref.shape[0]
    width = fwd_ref.shape[1]
    part = width // groups
    out_width = parts_ref.shape[2] - part

    rows = slice(None)
    for start in range(0, out_width, 1024):
        columns = slice(start, start + 1024)
        layer = parts_ref[0, rows, columns].astype(F32)
        for group in range(1, groups):
            layer += parts_ref[group, rows, columns].astype(F32)
        next_ref[0, rows, columns] = (fwd_ref[rows, columns].astype(F32) + layer).astype(BF16)
    next_ref[0, rows, out_width:] = fwd_ref[rows, out_width:]
    squares, inner = 0.0, 0.0
    for group in range(groups):
        columns = slice(group * part, (group + 1) * part)
        wide = bwd_ref[rows, columns].astype(F32)
        scaled = parts_ref[group, rows, out_width:].astype(F32) * gain_ref[:, columns]
        squares += jnp.sum(wide * wide, axis=1, keepdims=True)
        inner += jnp.sum(scaled * wide, axis=1, keepdims=True)
    scale = lax.rsqrt(squares * (1.0 / width) + EPS)
    pull = scale**3 * (inner * (1.0 / width))
    for group in range(groups):
        columns = slice(group * part, (group + 1) * part)
        wide = bwd_ref[rows, columns].astype(F32)
        scaled = parts_ref[group, rows, out_width:].astype(F32) * gain_ref[:, columns]
        out = grad_ref[rows, columns].astype(F32) + scale * scaled - wide * pull
        back_ref[0, rows, columns] = out.astype(BF16)


def update_kernel(
    entries, terms_ref, turned_ref, grad_ref, fwd_ref, back_ref, out_ref, next_ref, last_ref
):
    terms = terms_ref[...]
    total = jnp.sum(jnp.sum(terms, axis=0, keepdims=True)[:, :1], axis=1, keepdims=True)
    ratio = jnp.sqrt(entries / total)
    out_ref[...] = (ratio * dot(turned_ref[...], grad_ref[...], precision=None)).astype(BF16)
    next_ref[...] = fwd_ref[...]
    last_ref[...] = back_ref[...]


def per_device(x_fwd, x_bwd, grad_in, gain, weight, damping):
    fwd = x_fwd[0]
    bwd = x_bwd[0]
    grad = grad_in[0]
    local_w = weight[0]
    tokens, width = fwd.shape
    own_rows, out_width = local_w.shape
    groups = lax.axis_size("dp")
    group = groups * tokens
    me = lax.axis_index("dp")
    me_value = me.reshape(1, 1)
    damp_value = damping.reshape(1, 1)

    upstream = grad[:, :out_width]
    half = groups // 2
    other = swap(upstream, half)
    (sent,) = run(
        normalize_kernel,
        "normalize",
        [shape(groups, tokens, BLOCK + own_rows)],
        (),
        (fwd, bwd, gain),
        10**7,
    )
    sent, other = lax.optimization_barrier((sent, other))
    pair = jnp.concatenate([upstream, other], axis=0)
    near, far = swap(pair, 1), swap(pair, half - 1)
    rows = lax.all_to_all(sent, "dp", 0, 0, tiled=True).reshape(group, BLOCK + own_rows)

    left, *moves = solve_act(damp_value, me_value, rows)
    near, far, _ = lax.optimization_barrier((near, far, left))
    pieces = [pair, near, far, swap(far[:tokens], 1), swap(near[tokens:], half - 1)]
    columns = 512
    forward = pl.pallas_call(
        forward_kernel,
        grid=(out_width // columns,),
        out_shape=shape(groups, tokens, out_width + own_rows),
        in_specs=[
            pl.BlockSpec((group, BLOCK + own_rows), lambda i: (0, 0)),
            VMEM,
        ],
        out_specs=pl.BlockSpec((groups, tokens, columns), lambda i: (0, 0, i)),
        compiler_params=params(20),
        cost_estimate=cost(2 * 10**9, 8 * 10**6),
        name="forward",
    )(rows, local_w)
    scalar, *arrays = lax.optimization_barrier((me_value, *pieces, forward, left))[:-1]
    arrays = arrays[:-1] + [local_w, arrays[-1]]
    keep = pl.BlockSpec(memory_space=pl.ANY)
    outs = (shape(group, out_width), shape(groups, tokens, out_width + own_rows))
    group_grad, products = pl.pallas_call(
        product_kernel,
        grid=(1,),
        out_shape=outs,
        in_specs=[SMEM] + [VMEM] * (len(arrays) - 1) + [keep],
        out_specs=(whole_block(outs[0]), keep),
        scratch_shapes=[
            pltpu.VMEM((groups, tokens, own_rows), BF16),
            pltpu.SemaphoreType.DMA,
        ],
        input_output_aliases={len(arrays): 1},
        compiler_params=params(20),
        cost_estimate=cost(2 * 10**9, 10**7),
        name="products",
    )(scalar, *arrays)
    parts = lax.all_to_all(products, "dp", 0, 0, tiled=True)

    moves = moves[:1] + [
        lax.ppermute(piece, "dp", pairs) for piece, pairs in zip(moves[1:], PAIRS[1:])
    ]
    (turned,) = run(
        assemble_kernel,
        "assemble",
        [shape(own_rows, group)],
        (me_value,),
        moves,
        10**7,
        [pltpu.VMEM((group, (2 * WINDOW + 2) * UNIT), BF16)],
    )

    grad_tilde, term = solve_grad(damp_value, group_grad, left)
    devices = lax.axis_size("section") * groups
    terms = lax.all_to_all(
        jnp.broadcast_to(term, (devices, 128)), ("section", "dp"), 0, 0, tiled=True
    )

    parts, _ = lax.optimization_barrier((parts, term))
    step = 16
    wide_block = pl.BlockSpec((step, width), lambda i: (i, 0))
    out_block = pl.BlockSpec((1, step, width), lambda i: (0, i, 0))
    out_f, out_b = pl.pallas_call(
        finish_kernel,
        grid=(tokens // step,),
        out_shape=(shape(1, tokens, width),) * 2,
        in_specs=[
            pl.BlockSpec((groups, step, out_width + own_rows), lambda i: (0, i, 0)),
            wide_block,
            wide_block,
            wide_block,
            pl.BlockSpec((1, width), lambda i: (0, 0)),
        ],
        out_specs=(out_block, out_block),
        compiler_params=params(),
        cost_estimate=cost(10**7, 8 * 10**6),
        name="finish",
    )(parts, fwd, bwd, grad, gain)
    next_fwd = from_behind(out_f, "section", 1)
    next_grad = from_behind(out_b, "section", -1)
    terms, next_fwd, next_grad = lax.optimization_barrier((terms, next_fwd, next_grad))

    entries = float(lax.axis_size("section") * width * out_width)
    steps = 4
    columns = out_width // steps
    same = pl.BlockSpec((1, tokens, width // steps), lambda i: (0, 0, i))
    update, next_fwd, next_grad = pl.pallas_call(
        lambda *refs: update_kernel(entries, *refs),
        grid=(steps,),
        out_shape=(shape(own_rows, out_width),) + (shape(1, tokens, width),) * 2,
        in_specs=[
            pl.BlockSpec((devices, 128), lambda i: (0, 0)),
            pl.BlockSpec((own_rows, group), lambda i: (0, 0)),
            pl.BlockSpec((group, columns), lambda i: (0, i)),
            same,
            same,
        ],
        out_specs=(pl.BlockSpec((own_rows, columns), lambda i: (0, i)), same, same),
        compiler_params=params(),
        cost_estimate=cost(2 * 10**9, 8 * 10**6),
        name="update",
    )(terms, turned, grad_tilde, next_fwd, next_grad)
    return (next_fwd, next_grad, update[None])


def solution(mesh):
    return jax.shard_map(
        per_device,
        mesh=mesh,
        in_specs=(
            P("section", "dp", None),
            P("section", "dp", None),
            P("section", "dp", None),
            P("section", None),
            P("section", "dp", None),
            P("section"),
        ),
        out_specs=(P("section", "dp", None), P("section", "dp", None), P("section", "dp", None)),
        check_vma=False,
    )
```

```python
import jax
import jax.numpy as jnp
from jax import lax
from jax.experimental import pallas as pl
from jax.experimental.pallas import tpu as pltpu
from jax.sharding import PartitionSpec as P

BLOCK = 1024
EPS = 1e-06
F32 = jnp.float32
BF16 = jnp.bfloat16
EXACT = lax.Precision.HIGHEST


def dot(a, b, contract=(1, 0), precision=EXACT):
    return lax.dot_general(
        a,
        b,
        (((contract[0],), (contract[1],)), ((), ())),
        precision=precision,
        preferred_element_type=F32,
    )


def from_behind(value, axis, steps):
    count = lax.axis_size(axis)
    leading, last = (max(0, -steps), min(count, count - steps))
    return lax.ppermute(value, axis, [(source, source + steps) for source in range(leading, last)])


def normalize(x, gain):
    wide = x.astype(F32)
    scale = lax.rsqrt(jnp.mean(wide * wide, axis=-1, keepdims=True) + EPS)
    return ((wide * scale * gain).astype(BF16), scale)


def eye_mask(order):
    rows = lax.broadcasted_iota(jnp.int32, (order, order), 0)
    return rows == lax.broadcasted_iota(jnp.int32, (order, order), 1)


def step_coefficients(low, high):
    mid, half = (low + high) * 0.5, (high - low) * 0.5
    scale = 1.0 / (2.0 * mid * mid - half * half)
    return 4.0 * mid * scale, 2.0 * scale, half * half * scale


def split(value):
    high = value.astype(BF16)
    rest = value - high.astype(F32)
    middle = rest.astype(BF16)
    return high, middle, (rest - middle.astype(F32)).astype(BF16)


def dot_three(a, b):
    a_high, a_low, _ = split(a)
    b_high, b_low, _ = split(b)
    low = dot(a_low, b_high, precision=None) + dot(a_high, b_low, precision=None)
    return low + dot(a_high, b_high, precision=None)


def fourth_root(square):
    return jnp.sqrt(jnp.sqrt(jnp.sum(square * square)))


def by_rows(count, step, body):
    def one(index, carry):
        body(pl.ds(pl.multiple_of(index * step, step), step))
        return carry

    lax.fori_loop(0, count // step, one, 0)


def scaled_newton(spread, step):
    def once(spread):
        first, second, after = step_coefficients(1.0 - spread, 1.0 + spread)
        step(first, second)
        return after

    lax.while_loop(lambda spread: spread > 2e-2, once, spread)


def invert(matrix, low, state):
    order = matrix.shape[0]
    eye = eye_mask(order).astype(F32)
    square = dot(matrix, matrix)
    high = jnp.maximum(fourth_root(square), low) * 1.001
    first, second, spread = step_coefficients(low, high)
    state[:order] = first * eye - second * matrix
    state[order:] = first * matrix - second * square

    def step(first, second):
        both = state[...]
        state[...] = first * both - second * dot_three(both, both[order:])

    scaled_newton(spread, step)
    guess = state[:order]
    return guess + dot_three(guess, eye - dot(matrix, guess))


def invert_by_halves(factor, damping, state, parts):
    half = factor.shape[0] // 2
    parts[0] = factor[:half, :half]

    def stage(index, carry):
        inverse = invert(parts[index], damping, state)

        @pl.when(index == 0)
        def _():
            corner, upper = parts[0], factor[:half, half:]
            tall = dot(inverse, upper)

            parts[3] = tall - dot(inverse, dot(corner, tall) - upper)
            tall = parts[3]
            error = dot(corner, tall) - upper
            parts[1] = factor[half:, half:] - dot(tall.T, upper - error)

            parts[2] = inverse

        @pl.when(index == 1)
        def _():
            parts[1] = inverse

        return carry

    lax.fori_loop(0, 2, stage, 0)
    inverse, tall, rest = parts[2], parts[3], parts[1]
    cross = dot(tall, rest)
    factor[:half, :half] = inverse + dot(cross, tall.T)
    factor[:half, half:] = -cross
    factor[half:, :half] = -cross.T
    factor[half:, half:] = rest


def invert_whole(factor, damping, whole, spare):
    order = factor.shape[0]
    eye = eye_mask(order).astype(F32)

    def square(rows):
        spare[rows] = dot(factor[rows], factor[...])

    by_rows(order, 128, square)
    high = jnp.maximum(fourth_root(spare[...]), damping) * 1.001
    first, second, spread = step_coefficients(damping, high)
    whole[:order] = first * eye - second * factor[...]
    whole[order:] = first * factor[...] - second * spare[...]

    def step(first, second):
        spare[...] = whole[order:]

        def some(rows):
            whole[rows] = first * whole[rows] - second * dot(whole[rows], spare[...])

        by_rows(2 * order, 128, some)

    scaled_newton(spread, step)

    def polish(_, carry):
        def residual(rows):
            spare[rows] = dot(factor[rows], whole[:order])

        by_rows(order, 128, residual)
        spare[...] = eye - spare[...]

        def correct(rows):
            whole[rows] += dot(whole[rows], spare[...])

        by_rows(order, 128, correct)
        return carry

    lax.fori_loop(0, 3, polish, 0)


def apply_inverse(damping, rows_ref, columns, out_ref, out_columns, scratch):
    factor, state, parts, whole, spare = scratch
    count = rows_ref.shape[0]
    half = count // 2
    width = 256

    def gram(rows):
        factor[rows] = dot(rows_ref[rows, columns(0, BLOCK)], rows_ref[:, columns(0, BLOCK)], (1, 1), None) * (
            1.0 / count
        )

    by_rows(count, half, gram)
    squares = []
    for corner in (factor[:half, :half], factor[half:, half:]):
        corner = corner.astype(BF16)
        squares.append(jnp.abs(dot(corner, corner, precision=None)))
    easy = fourth_root(jnp.maximum(*squares)) < HARDEST * damping
    factor[...] = jnp.where(eye_mask(count), factor[...] + damping, factor[...])

    @pl.when(easy)
    def _():
        invert_by_halves(factor, damping, state, parts)

        def solve(rows):
            high, low, _ = split(factor[rows])
            block = rows_ref[:, columns(0, BLOCK)]
            solved = dot(low, block, precision=None) + dot(high, block, precision=None)
            out_ref[rows, out_columns(0, BLOCK)] = solved.astype(BF16)

        by_rows(count, half, solve)

    @pl.when(jnp.logical_not(easy))
    def _():
        invert_whole(factor, damping, whole, spare)

        def solve(index, carry):
            start = index * width
            exact = rows_ref[:, columns(start, width)].astype(F32)

            def guess(rows):
                spare[rows, :width] = dot(whole[rows], exact)

            def residual(rows):
                spare[rows, width:] = dot(factor[rows], spare[:, :width])

            def correct(rows):
                fixed = spare[rows, :width] + dot(whole[rows], spare[:, width:])
                out_ref[rows, out_columns(start, width)] = fixed.astype(BF16)

            by_rows(count, 128, guess)
            by_rows(count, 128, residual)
            spare[:, width:] = exact - spare[:, width:]
            by_rows(count, 128, correct)
            return carry

        lax.fori_loop(0, BLOCK // width, solve, 0)


HARDEST = 2e4


def solver_scratch(count):
    half = count // 2
    return [
        pltpu.VMEM((count, count), F32),
        pltpu.VMEM((count, half), F32),
        pltpu.VMEM((4, half, half), F32),
        pltpu.VMEM((2 * count, count), F32),
        pltpu.VMEM((count, count), F32),
    ]


OWNERS = (0, 2, 4, 5, 7)
UNIT = 128
MOVES = (
    (5, {0: 0, 2: 2, 4: 3, 5: 1, 7: 3}, {0: 0, 2: 0, 4: -1, 5: 0, 7: 0}),
    (4, {0: 4, 4: 0, 7: 0}, {1: -1, 3: 1, 6: 2}),
    (2, {2: 0, 5: 6}, {1: 3, 6: 0}),
    (1, {2: 7, 5: 0}, {3: 0, 4: 4}),
)
PAIRS = (None, ((0, 1), (4, 3), (7, 6)), ((2, 1), (5, 6)), ((2, 3), (5, 4)))
WINDOW = 5


def lookup(table, missing, me):
    value = jnp.int32(missing)
    for device, entry in table.items():
        value = jnp.where(me == device, entry, value)
    return value


def act_kernel(damping_ref, me_ref, rows_ref, left_ref, *refs):
    moves, (solved_ref, *scratch) = refs[: len(MOVES)], refs[len(MOVES) :]

    def columns(start, size):
        return slice(start, start + size) if isinstance(start, int) else pl.ds(start, size)

    apply_inverse(damping_ref[0, 0], rows_ref, columns, solved_ref, columns, scratch)

    def compare(rows):
        left_ref[rows] = dot(solved_ref[rows, :], rows_ref[:, :BLOCK], (1, 1), None)

    by_rows(solved_ref.shape[0], 256, compare)
    for (units, first, _), out in zip(MOVES, moves):
        start = pl.multiple_of(lookup(first, 0, me_ref[0, 0]) * UNIT, UNIT)
        out[...] = solved_ref[:, pl.ds(start, units * UNIT)]


def assemble_kernel(me_ref, *refs):
    moves, (out_ref, buffer) = refs[: len(MOVES)], refs[len(MOVES) :]
    for (units, _, place), piece in zip(MOVES, moves):
        start = (lookup(place, WINDOW + 1, me_ref[0, 0]) + 1) * UNIT
        buffer[:, pl.ds(pl.multiple_of(start, UNIT), units * UNIT)] = piece[...]
    out_ref[...] = buffer[:, UNIT : (WINDOW + 1) * UNIT].T


def grad_kernel(damping_ref, rows_ref, left_ref, solved_ref, term_ref, right, *scratch):
    count, width = rows_ref.shape

    def one(index, carry):
        def columns(start, size):
            return pl.ds(pl.multiple_of(index * BLOCK + start, UNIT), size)

        apply_inverse(damping_ref[0, 0], rows_ref, columns, solved_ref, columns, scratch)
        return carry

    lax.fori_loop(0, width // BLOCK, one, 0)

    def compare(rows):
        product = dot(solved_ref[rows, :], rows_ref[...], (1, 1), None)
        right[rows] = product * left_ref[rows]

    by_rows(count, 256, compare)
    product = jnp.sum(right[...], axis=0, keepdims=True)
    term_ref[...] = jnp.broadcast_to(jnp.sum(product, axis=1, keepdims=True), term_ref.shape)


SMEM = pl.BlockSpec(memory_space=pltpu.SMEM)
VMEM = pl.BlockSpec(memory_space=pltpu.VMEM)


def shape(*dims, dtype=BF16):
    return jax.ShapeDtypeStruct(dims, dtype)


def whole_block(value):
    return pl.BlockSpec(value.shape, lambda i: (0,) * len(value.shape))


def cost(flops, moved):
    return pl.CostEstimate(flops=flops, bytes_accessed=moved, transcendentals=0)


def params(mib=56):
    return pltpu.CompilerParams(vmem_limit_bytes=mib * 2**20)


def run(kernel, name, outs, scalars, arrays, flops, scratch=(), mib=56):
    moved = sum(value.size * value.dtype.itemsize for value in (*arrays, *outs))
    return pl.pallas_call(
        kernel,
        grid=(1,),
        out_shape=tuple(outs),
        in_specs=[SMEM] * len(scalars) + [whole_block(value) for value in arrays],
        out_specs=tuple(whole_block(value) for value in outs),
        scratch_shapes=list(scratch),
        compiler_params=params(mib),
        cost_estimate=cost(flops, moved),
        name=name,
    )(*scalars, *arrays)


def solve_act(damping, me, rows):
    count = rows.shape[0]
    outs = [shape(count, count, dtype=F32)]
    outs += [shape(count, units * UNIT) for units, _, _ in MOVES]
    scratch = [pltpu.VMEM((count, BLOCK), BF16)] + solver_scratch(count)
    return run(act_kernel, "solve_act", outs, (damping, me), (rows,), 16 * 10**9, scratch, 28)


def solve_grad(damping, rows, left, devices):
    count, width = rows.shape
    outs = [shape(count, width), shape(devices, UNIT, dtype=F32)]
    scratch = [pltpu.VMEM((count, count), F32)] + solver_scratch(count)
    return run(grad_kernel, "solve_grad", outs, (damping,), (rows, left), 45 * 10**9, scratch)


def swap(value, offset):
    return lax.ppermute(value, "dp", [(i, i ^ offset) for i in range(8)])


def normalize_kernel(fwd_ref, bwd_ref, gain_ref, out_ref):
    gain = gain_ref[...]
    normed_b, _ = normalize(bwd_ref[...], gain)
    normed_f, _ = normalize(fwd_ref[...], gain)
    part = normed_f.shape[1] // out_ref.shape[0]
    for device in range(out_ref.shape[0]):
        if device in OWNERS:
            block = OWNERS.index(device)
            out_ref[device, :, :BLOCK] = normed_b[:, block * BLOCK : (block + 1) * BLOCK]
        else:
            out_ref[device, :, :BLOCK] = jnp.zeros((normed_b.shape[0], BLOCK), BF16)
        out_ref[device, :, BLOCK:] = normed_f[:, device * part : (device + 1) * part]


def forward_kernel(rows_ref, weight_ref, out_ref):
    width = out_ref.shape[2]
    columns = pl.ds(pl.multiple_of(pl.program_id(0) * width, width), width)
    forward = dot(rows_ref[:, BLOCK:], weight_ref[:, columns], precision=None)
    out_ref[...] = forward.astype(BF16).reshape(out_ref.shape)


HELD = ((0, 4), (1, 5), (3, 7), (2,), (6,))


def product_kernel(me_ref, *refs):
    me = me_ref[0, 0]
    pieces, (weight_ref, _, gathered, out_ref, back, sem) = refs[: len(HELD)], refs[len(HELD) :]
    groups, tokens, part = back.shape
    for held, piece in zip(HELD, pieces):
        for index, offset in enumerate(held):
            start = pl.multiple_of((me ^ offset) * tokens, tokens)
            gathered[pl.ds(start, tokens), :] = piece[index * tokens : (index + 1) * tokens, :]
    backward = dot(gathered[...], weight_ref[...], (1, 1), None)
    back[...] = backward.astype(BF16).reshape(groups, tokens, part)
    copy = pltpu.make_async_copy(back, out_ref.at[:, :, pl.ds(weight_ref.shape[1], part)], sem)
    copy.start()
    copy.wait()


def finish_kernel(parts_ref, fwd_ref, bwd_ref, grad_ref, gain_ref, next_ref, back_ref):
    groups = parts_ref.shape[0]
    width = fwd_ref.shape[1]
    part = width // groups
    out_width = parts_ref.shape[2] - part

    rows = slice(None)
    for start in range(0, out_width, 1024):
        columns = slice(start, start + 1024)
        layer = parts_ref[0, rows, columns].astype(F32)
        for group in range(1, groups):
            layer += parts_ref[group, rows, columns].astype(F32)
        next_ref[0, rows, columns] = (fwd_ref[rows, columns].astype(F32) + layer).astype(BF16)
    next_ref[0, rows, out_width:] = fwd_ref[rows, out_width:]
    squares, inner = 0.0, 0.0
    for group in range(groups):
        columns = slice(group * part, (group + 1) * part)
        wide = bwd_ref[rows, columns].astype(F32)
        scaled = parts_ref[group, rows, out_width:].astype(F32) * gain_ref[:, columns]
        squares += jnp.sum(wide * wide, axis=1, keepdims=True)
        inner += jnp.sum(scaled * wide, axis=1, keepdims=True)
    scale = lax.rsqrt(squares * (1.0 / width) + EPS)
    pull = scale**3 * (inner * (1.0 / width))
    for group in range(groups):
        columns = slice(group * part, (group + 1) * part)
        wide = bwd_ref[rows, columns].astype(F32)
        scaled = parts_ref[group, rows, out_width:].astype(F32) * gain_ref[:, columns]
        out = grad_ref[rows, columns].astype(F32) + scale * scaled - wide * pull
        back_ref[0, rows, columns] = out.astype(BF16)


def update_kernel(
    entries, terms_ref, turned_ref, grad_ref, fwd_ref, back_ref, out_ref, next_ref, last_ref, held
):
    step = pl.program_id(0)

    def columns(width):
        return pl.ds(pl.multiple_of(step * width, width), width)

    @pl.when(step == 0)
    def _():
        terms = jnp.sum(terms_ref[...], axis=0, keepdims=True)[:, :1]
        held[...] = jnp.broadcast_to(jnp.sqrt(entries / terms), held.shape)

    ratio = held[:1, :1]
    precond = dot(turned_ref[...], grad_ref[:, columns(out_ref.shape[1])], precision=None)
    out_ref[...] = (ratio * precond).astype(BF16)
    width = next_ref.shape[2]
    next_ref[...] = fwd_ref[:, :, columns(width)]
    last_ref[...] = back_ref[:, :, columns(width)]


def per_device(x_fwd, x_bwd, grad_in, gain, weight, damping):
    fwd = x_fwd[0]
    bwd = x_bwd[0]
    grad = grad_in[0]
    local_w = weight[0]
    tokens, width = fwd.shape
    own_rows, out_width = local_w.shape
    groups = lax.axis_size("dp")
    group = groups * tokens
    me = lax.axis_index("dp")
    me_value = me.reshape(1, 1)
    damp_value = damping.reshape(1, 1)

    upstream = grad[:, :out_width]
    half = groups // 2
    other = swap(upstream, half)
    (sent,) = run(
        normalize_kernel,
        "normalize",
        [shape(groups, tokens, BLOCK + own_rows)],
        (),
        (fwd, bwd, gain),
        10**7,
    )
    sent, other = lax.optimization_barrier((sent, other))
    pair = jnp.concatenate([upstream, other], axis=0)
    near, far = swap(pair, 1), swap(pair, half - 1)
    rows = lax.all_to_all(sent, "dp", 0, 0, tiled=True).reshape(group, BLOCK + own_rows)

    left, *moves = solve_act(damp_value, me_value, rows)
    near, far, _ = lax.optimization_barrier((near, far, left))
    pieces = [pair, near, far, swap(far[:tokens], 1), swap(near[tokens:], half - 1)]
    columns = 512
    forward = pl.pallas_call(
        forward_kernel,
        grid=(out_width // columns,),
        out_shape=shape(groups, tokens, out_width + own_rows),
        in_specs=[
            pl.BlockSpec((group, BLOCK + own_rows), lambda i: (0, 0)),
            VMEM,
        ],
        out_specs=pl.BlockSpec((groups, tokens, columns), lambda i: (0, 0, i)),
        compiler_params=params(20),
        cost_estimate=cost(2 * 10**9, 8 * 10**6),
        name="forward",
    )(rows, local_w)
    scalar, *arrays = lax.optimization_barrier((me_value, *pieces, forward, left))[:-1]
    arrays = arrays[:-1] + [local_w, arrays[-1]]
    keep = pl.BlockSpec(memory_space=pl.ANY)
    outs = (shape(group, out_width), shape(groups, tokens, out_width + own_rows))
    group_grad, products = pl.pallas_call(
        product_kernel,
        grid=(1,),
        out_shape=outs,
        in_specs=[SMEM] + [VMEM] * (len(arrays) - 1) + [keep],
        out_specs=(whole_block(outs[0]), keep),
        scratch_shapes=[
            pltpu.VMEM((groups, tokens, own_rows), BF16),
            pltpu.SemaphoreType.DMA,
        ],
        input_output_aliases={len(arrays): 1},
        compiler_params=params(20),
        cost_estimate=cost(2 * 10**9, 10**7),
        name="products",
    )(scalar, *arrays)
    parts = lax.all_to_all(products, "dp", 0, 0, tiled=True)

    moves = moves[:1] + [
        lax.ppermute(piece, "dp", pairs) for piece, pairs in zip(moves[1:], PAIRS[1:])
    ]
    (turned,) = run(
        assemble_kernel,
        "assemble",
        [shape(own_rows, group)],
        (me_value,),
        moves,
        10**7,
        [pltpu.VMEM((group, (2 * WINDOW + 2) * UNIT), BF16)],
    )

    devices = lax.axis_size("section") * groups
    grad_tilde, term = solve_grad(damp_value, group_grad, left, devices)
    terms = lax.all_to_all(term, ("section", "dp"), 0, 0, tiled=True)

    parts, _ = lax.optimization_barrier((parts, term))
    step = 16
    wide_block = pl.BlockSpec((step, width), lambda i: (i, 0))
    out_block = pl.BlockSpec((1, step, width), lambda i: (0, i, 0))
    out_f, out_b = pl.pallas_call(
        finish_kernel,
        grid=(tokens // step,),
        out_shape=(shape(1, tokens, width),) * 2,
        in_specs=[
            pl.BlockSpec((groups, step, out_width + own_rows), lambda i: (0, i, 0)),
            wide_block,
            wide_block,
            wide_block,
            pl.BlockSpec((1, width), lambda i: (0, 0)),
        ],
        out_specs=(out_block, out_block),
        compiler_params=params(),
        cost_estimate=cost(10**7, 8 * 10**6),
        name="finish",
    )(parts, fwd, bwd, grad, gain)
    next_fwd = from_behind(out_f, "section", 1)
    next_grad = from_behind(out_b, "section", -1)
    terms, next_fwd, next_grad = lax.optimization_barrier((terms, next_fwd, next_grad))

    entries = float(lax.axis_size("section") * width * out_width)
    steps = 4
    columns = out_width // steps
    same = pl.BlockSpec((1, tokens, width // steps), lambda i: (0, 0, i))
    update, next_fwd, next_grad = pl.pallas_call(
        lambda *refs: update_kernel(entries, *refs),
        grid=(steps,),
        out_shape=(shape(own_rows, out_width),) + (shape(1, tokens, width),) * 2,
        in_specs=[pl.BlockSpec((devices, 128), lambda i: (0, 0))] + [VMEM] * 4,
        out_specs=(pl.BlockSpec((own_rows, columns), lambda i: (0, i)), same, same),
        scratch_shapes=[pltpu.VMEM((8, 128), F32)],
        compiler_params=params(20),
        cost_estimate=cost(2 * 10**9, 8 * 10**6),
        name="update",
    )(terms, turned, grad_tilde, next_fwd, next_grad)
    return (next_fwd, next_grad, update[None])


def solution(mesh):
    return jax.shard_map(
        per_device,
        mesh=mesh,
        in_specs=(
            P("section", "dp", None),
            P("section", "dp", None),
            P("section", "dp", None),
            P("section", None),
            P("section", "dp", None),
            P("section"),
        ),
        out_specs=(P("section", "dp", None), P("section", "dp", None), P("section", "dp", None)),
        check_vma=False,
    )
```
